256 devices in a mesh: grp: 8 (over x, y_lo), mem: 32 (over z, y_hi, core).
Axes of the slice: x: 4, y: 4 (y_hi: 2, y_lo: 2; y = y_hi * 2 + y_lo), z: 8, core: 2. Of those that a mesh axis runs over, the one named last changes fastest.
Arguments:
- image_embed: bfloat16 [20480, 1280], P(('mem', 'grp')), may hold values from -0.6 to 0.6
- text_embed: bfloat16 [20480, 1280], P(('grp', 'mem')), may hold values from -0.6 to 0.6
- pair_index: int32 [20480], P(('mem', 'grp')), may hold values from 0 to 20479, each once
Outputs:
- grad_image: bfloat16 [20480, 1280], P(('mem', 'grp'))
- grad_text: bfloat16 [20480, 1280], P(('grp', 'mem'))
- mean_loss: float32 [], replicated
The draws below stay inside these ranges and needn't reach their ends.
Inputs may be any that keep to these rules, and one draw needn't show every extreme that they name: Image row i is paired with text row pair_index[i]; every text row is paired with exactly one image row.
All inputs are finite; a program needn't handle non-finite values.
Results may differ from the reference program's by a relative error of at most 0.015.
Values may be sent and summed in bfloat16 or wider, within the bound.
No kernel may reach another device: no remote copies, remote signals or barrier semaphores. Data moves between devices by JAX's collectives and lax.ppermute only.
A program may use at most 64 MiB of HBM per device.

```python
import jax
import jax.numpy as jnp
from jax import lax

E = 1280
TOTAL = 20480
N_GRP = 8
N_MEM = 32


def spread_rows(base_rows, scale_key):
    position = jnp.arange(TOTAL, dtype=jnp.float32)
    row_trend = 0.5 + position / TOTAL
    spread = jnp.power(10.0, jax.random.uniform(scale_key, (TOTAL,), jnp.float32) - 0.5)
    return 0.02 * base_rows * (spread * row_trend)[:, None]


def draw_image_embed(key, part):
    key = jax.random.fold_in(key, 3)
    base_key, scale_key = jax.random.split(key, 2)
    values = spread_rows(jax.random.normal(base_key, (TOTAL, E), jnp.float32), scale_key)
    return jnp.clip(values, -0.6, 0.6).astype(jnp.bfloat16)


def draw_text_embed(key, part):
    key = jax.random.fold_in(key, 5)
    base_key, scale_key = jax.random.split(key, 2)
    values = spread_rows(jax.random.normal(base_key, (TOTAL, E), jnp.float32), scale_key)
    return jnp.clip(values, -0.6, 0.6).astype(jnp.bfloat16)


def setup_inputs(seed: int = 0) -> dict:
    arg_keys = jax.random.split(jax.random.key(seed), 4)
    image_embed = draw_image_embed(jax.random.fold_in(arg_keys[3], 71), 0)
    text_embed = draw_text_embed(jax.random.fold_in(arg_keys[3], 71), 0)
    pair_index = jax.random.permutation(arg_keys[2], TOTAL).astype(jnp.int32)
    return dict(image_embed=image_embed, text_embed=text_embed, pair_index=pair_index)


LOGIT_SCALE = 100.0


def reference(image_embed, text_embed, pair_index):
    block_rows = TOTAL // N_MEM
    group_cols = TOTAL // N_GRP
    image_blocks = image_embed.reshape(N_MEM, block_rows, E)
    pair_blocks = pair_index.reshape(N_MEM, block_rows)
    columns = jnp.arange(TOTAL, dtype=jnp.int32)
    text_groups = text_embed.reshape(N_GRP, group_cols, E).astype(jnp.float32)

    def scores_of(image_rows):
        return LOGIT_SCALE * jnp.dot(image_rows, text_embed.T, preferred_element_type=jnp.float32)

    def first_pass(running, inputs):
        col_peak, col_total, positive = running
        image_rows, targets = inputs
        scores = scores_of(image_rows)
        row_peak = jnp.max(scores, axis=1)
        row_logsum = row_peak + jnp.log(jnp.sum(jnp.exp(scores - row_peak[:, None]), axis=1))
        new_peak = jnp.maximum(col_peak, jnp.max(scores, axis=0))
        col_total = col_total * jnp.exp(col_peak - new_peak) + jnp.sum(jnp.exp(scores - new_peak[None, :]), axis=0)
        matches = targets[:, None] == columns[None, :]
        positive = positive + jnp.sum(jnp.where(matches, scores, jnp.float32(0.0)))
        return (new_peak, col_total, positive), row_logsum

    initial = (jnp.full((TOTAL,), -jnp.inf, jnp.float32), jnp.zeros((TOTAL,), jnp.float32), jnp.float32(0.0))
    (col_peak, col_total, positive), row_logsum = lax.scan(first_pass, initial, (image_blocks, pair_blocks))
    col_logsum = col_peak + jnp.log(col_total)
    mean_loss = (jnp.sum(row_logsum) + jnp.sum(col_logsum) - 2.0 * positive) / (2.0 * TOTAL)

    def second_pass(text_grad, inputs):
        image_rows, targets, row_part = inputs
        scores = scores_of(image_rows)
        matches = (targets[:, None] == columns[None, :]).astype(jnp.float32)
        grad_logits = (0.5 * (jnp.exp(scores - row_part[:, None]) + jnp.exp(scores - col_logsum[None, :])) - matches).astype(jnp.bfloat16)
        grouped = grad_logits.reshape(block_rows, N_GRP, group_cols).astype(jnp.float32)
        image_part = (LOGIT_SCALE * jnp.einsum("rgc,gce->gre", grouped, text_groups)).astype(jnp.bfloat16)
        image_part = lax.optimization_barrier(image_part)
        grad_rows = jnp.sum(image_part.astype(jnp.float32), axis=0).astype(jnp.bfloat16)
        text_part = (LOGIT_SCALE * jnp.dot(grad_logits.T, image_rows, preferred_element_type=jnp.float32)).astype(jnp.bfloat16)
        text_part = lax.optimization_barrier(text_part)
        text_grad = text_grad + text_part.astype(jnp.float32)
        return text_grad, grad_rows

    text_grad, grad_rows = lax.scan(second_pass, jnp.zeros((TOTAL, E), jnp.float32), (image_blocks, pair_blocks, row_logsum))
    return grad_rows.reshape(TOTAL, E), text_grad.astype(jnp.bfloat16), mean_loss
```

```python
import jax
import jax.numpy as jnp
import numpy as np
from jax import lax
from jax.experimental import pallas as pl
from jax.experimental.pallas import tpu as pltpu
from jax.sharding import Mesh, PartitionSpec as P

LOGIT_SCALE = 100.0
AXES = ("x", "yl", "z", "yh", "core")
SIZES = (4, 2, 8, 2, 2)
CHUNK = 80
WIDTH = 1280
HALF = WIDTH // 2
SIDE = 16 * CHUNK
COL_STEP = 256
ROW_STEP = 128
VMEM = 56 * 1024 * 1024


def moves(dx=0, dy=0, dz=0, dc=0):
    out = []
    for x, yl, z, yh, c in np.ndindex(*SIZES):
        y = (yh * 2 + yl + dy) % 4
        to = ((x + dx) % 4, y % 2, (z + dz) % 8, y // 2, (c + dc) % 2)
        out.append(
            (int(np.ravel_multi_index((x, yl, z, yh, c), SIZES)), int(np.ravel_multi_index(to, SIZES)))
        )
    return out


def shift(value, **step):
    return lax.ppermute(value, AXES, moves(**step))


def as_columns(row):
    return jnp.transpose(jnp.broadcast_to(row, (128, SIDE)))


def dot_t(a, b):
    return lax.dot_general(a, b, (((1,), (1,)), ((), ())), preferred_element_type=jnp.float32)


def scores_kernel(ip, iq, t, s_ref, row_ref, col_ref, peak, total):
    def block(j, _):
        cols = pl.ds(pl.multiple_of(j * COL_STEP, COL_STEP), COL_STEP)
        s = dot_t(ip[...], t[cols, :HALF]) + dot_t(iq[...], t[cols, HALF:])
        s = LOGIT_SCALE * s
        s_ref[:, cols] = s
        col_ref[0:1, cols] = jnp.max(s, axis=0, keepdims=True)
        lanes = s[:, :128]
        for k in range(1, COL_STEP // 128):
            lanes = jnp.maximum(lanes, s[:, k * 128 : (k + 1) * 128])

        @pl.when(j == 0)
        def _():
            peak[...] = lanes

        @pl.when(j > 0)
        def _():
            peak[...] = jnp.maximum(peak[...], lanes)

        return 0

    lax.fori_loop(0, SIDE // COL_STEP, block, 0)
    row_peak = jnp.max(jnp.transpose(peak[...]), axis=0, keepdims=True)
    row_ref[0:1, :] = row_peak
    peak[...] = as_columns(row_peak)
    col_ref[1:2, :] = jnp.zeros((1, SIDE), jnp.float32)

    def sums(i, _):
        rows = pl.ds(pl.multiple_of(i * ROW_STEP, ROW_STEP), ROW_STEP)
        m = peak[rows, :]
        acc = jnp.zeros((ROW_STEP, 128), jnp.float32)
        for k in range(SIDE // 128):
            cols = slice(k * 128, (k + 1) * 128)
            s = s_ref[rows, cols]
            acc = acc + jnp.exp(s - m)
            q = jnp.exp(s - col_ref[0:1, cols])
            col_ref[1:2, cols] += jnp.sum(q, axis=0, keepdims=True)
        total[rows, :] = acc
        return 0

    lax.fori_loop(0, SIDE // ROW_STEP, sums, 0)
    row_ref[1:2, :] = jnp.sum(jnp.transpose(total[...]), axis=0, keepdims=True)


def logits_kernel(s_ref, ip, iq, row_log, col_log, pairs, ids, g_ref, gt_ref, pos_ref, rows_log, rows_pair):
    rows_log[...] = as_columns(row_log[...])
    rows_pair[...] = as_columns(pairs[...])
    pos_ref[...] = jnp.zeros_like(pos_ref)

    def block(i, _):
        rows = pl.ds(pl.multiple_of(i * ROW_STEP, ROW_STEP), ROW_STEP)
        r = rows_log[rows, :]
        pr = rows_pair[rows, :]
        acc = jnp.zeros((ROW_STEP, 128), jnp.float32)
        for k in range(SIDE // 128):
            cols = slice(k * 128, (k + 1) * 128)
            s = s_ref[rows, cols]
            g = 0.5 * (jnp.exp(s - r) + jnp.exp(s - col_log[:, cols]))
            match = pr == ids[:, cols]
            acc = acc + jnp.where(match, s, 0.0)
            g_ref[rows, cols] = jnp.where(match, g - 1.0, g).astype(jnp.bfloat16)
        pos_ref[...] += jnp.sum(acc.reshape(ROW_STEP // 8, 8, 128), axis=0)
        return 0

    lax.fori_loop(0, SIDE // ROW_STEP, block, 0)

    def back(j, _):
        cols = pl.ds(pl.multiple_of(j * COL_STEP, COL_STEP), COL_STEP)
        g = g_ref[:, cols]
        for half, ref in ((0, ip), (1, iq)):
            out = lax.dot_general(g, ref[...], (((0,), (0,)), ((), ())), preferred_element_type=jnp.float32)
            gt_ref[cols, half * HALF : (half + 1) * HALF] = (LOGIT_SCALE * out).astype(jnp.bfloat16)
        return 0

    lax.fori_loop(0, SIDE // COL_STEP, back, 0)


def image_kernel(g_ref, t_ref, out_ref):
    def block(i, _):
        rows = pl.ds(pl.multiple_of(i * COL_STEP, COL_STEP), COL_STEP)
        out = jnp.dot(g_ref[rows, :], t_ref[...], preferred_element_type=jnp.float32)
        out_ref[rows, :] = (LOGIT_SCALE * out).astype(jnp.bfloat16)
        return 0

    lax.fori_loop(0, SIDE // COL_STEP, block, 0)


FLOPS = 2 * SIDE * SIDE * WIDTH
CALL = dict(compiler_params=pltpu.CompilerParams(vmem_limit_bytes=VMEM))


def whole(n):
    return [pl.BlockSpec(memory_space=pltpu.VMEM)] * n


def scores_call(ip, iq, t):
    f32 = jnp.float32
    return pl.pallas_call(
        scores_kernel,
        out_shape=(
            jax.ShapeDtypeStruct((SIDE, SIDE), f32),
            jax.ShapeDtypeStruct((2, SIDE), f32),
            jax.ShapeDtypeStruct((2, SIDE), f32),
        ),
        in_specs=whole(3),
        out_specs=tuple(whole(3)),
        scratch_shapes=[pltpu.VMEM((SIDE, 128), f32), pltpu.VMEM((SIDE, 128), f32)],
        cost_estimate=pl.CostEstimate(flops=FLOPS, bytes_accessed=13 << 20, transcendentals=2 * SIDE * SIDE),
        **CALL,
    )(ip, iq, t)


def logits_call(s, ip, iq, row_log, col_log, pairs, ids):
    f32 = jnp.float32
    return pl.pallas_call(
        logits_kernel,
        out_shape=(
            jax.ShapeDtypeStruct((SIDE, SIDE), jnp.bfloat16),
            jax.ShapeDtypeStruct((SIDE, WIDTH), jnp.bfloat16),
            jax.ShapeDtypeStruct((8, 128), f32),
        ),
        in_specs=whole(7),
        out_specs=tuple(whole(3)),
        scratch_shapes=[pltpu.VMEM((SIDE, 128), f32), pltpu.VMEM((SIDE, 128), f32)],
        cost_estimate=pl.CostEstimate(flops=FLOPS, bytes_accessed=16 << 20, transcendentals=2 * SIDE * SIDE),
        **CALL,
    )(s, ip, iq, row_log, col_log, pairs, ids)


def image_call(g, t):
    return pl.pallas_call(
        image_kernel,
        out_shape=jax.ShapeDtypeStruct((SIDE, WIDTH), jnp.bfloat16),
        in_specs=whole(2),
        out_specs=whole(1)[0],
        cost_estimate=pl.CostEstimate(flops=FLOPS, bytes_accessed=10 << 20, transcendentals=0),
        **CALL,
    )(g, t)


def ring_gather(first, axis, cut):
    a, b = cut(first)
    up, down = {axis: 1}, {axis: -1}
    a1, b3 = shift(a, **up), shift(b, **down)
    b1, a3 = shift(b, **up), shift(a, **down)
    a2, b2 = shift(a1, **up), shift(b3, **down)
    return [(a, b), (a1, b1), (a2, b2), (a3, b3)]


def direct_gather(own, axis):
    return [own, shift(own, **{axis: 1}), shift(own, **{axis: 2}), shift(own, **{axis: -1})]


def gather_image(image):
    own_p, own_q = image[:, :HALF], image[:, HALF:]
    px = direct_gather(own_p, "dx")
    qy = direct_gather(own_q, "dy")
    cut = lambda block: (block[:2], block[2:])
    p_all = ring_gather(jnp.stack(px), "dy", cut)
    q_all = ring_gather(jnp.stack(qy), "dx", cut)
    p = jnp.stack([jnp.concatenate(ab, axis=0) for ab in p_all], axis=1)
    q = jnp.stack([jnp.concatenate(ab, axis=0) for ab in q_all], axis=0)
    return p.reshape(SIDE, HALF), q.reshape(SIDE, HALF)


def f32(value):
    return value.astype(jnp.float32)


def ring_scatter(blocks, axis):
    up, down = {axis: 1}, {axis: -1}
    bf16 = jnp.bfloat16
    a2 = shift(blocks[2][0], **down)
    b2 = shift(blocks[2][1], **up)
    b1 = shift(blocks[1][1], **down)
    a3 = shift(blocks[3][0], **up)
    a1 = shift((f32(blocks[1][0]) + f32(a2)).astype(bf16), **down)
    b3 = shift((f32(blocks[3][1]) + f32(b2)).astype(bf16), **up)
    a = f32(blocks[0][0]) + f32(a1) + f32(a3)
    b = f32(blocks[0][1]) + f32(b1) + f32(b3)
    return jnp.concatenate([a, b], axis=0)


def direct_scatter(sums, axis):
    sent = sums.astype(jnp.bfloat16)
    from_up = shift(sent[1], **{axis: -1})
    from_down = shift(sent[3], **{axis: 1})
    from_far = shift(sent[2], **{axis: 2})
    return sums[0] + f32(from_up) + f32(from_down) + f32(from_far)


def scatter_image(grads):
    g = grads.reshape(4, 4, CHUNK, WIDTH)
    gp, gq = g[..., :HALF], g[..., HALF:]
    p_blocks = [(gp[:2, k], gp[2:, k]) for k in range(4)]
    q_blocks = [(gq[k, :2], gq[k, 2:]) for k in range(4)]
    p = direct_scatter(ring_scatter(p_blocks, "dy"), "dx")
    q = direct_scatter(ring_scatter(q_blocks, "dx"), "dy")
    return jnp.concatenate([p, q], axis=1).astype(jnp.bfloat16)


def merge(one, two):
    peak = jnp.maximum(one[0], two[0])
    total = one[1] * jnp.exp(one[0] - peak) + two[1] * jnp.exp(two[0] - peak)
    return peak, total


def reduce_rows(stats, pairs):
    mine = jnp.full((SIDE,), -1.0, jnp.float32).at[:CHUNK].set(pairs.astype(jnp.float32))
    state = jnp.stack([stats[0], stats[1], mine]).reshape(3, 4, 4, CHUNK)
    for axis, dim in (("dx", 1), ("dy", 2)):
        for step in (1, 2):
            other = jnp.roll(shift(state, **{axis: step}), step, axis=dim)
            peak, total = merge(state, other)
            state = jnp.stack([peak, total, jnp.maximum(state[2], other[2])])
    return state.reshape(3, SIDE)


def reduce_cols(stats):
    for step in (dict(dc=1), dict(dz=1), dict(dz=2), dict(dz=4)):
        stats = jnp.stack(merge(stats, shift(stats, **step)))
    return stats


def per_device(image, text, pairs):
    x, yl, z, yh, core = (lax.axis_index(name) for name in AXES)
    t = lax.all_gather(text, ("z", "core"), axis=0, tiled=True)
    ip, iq = gather_image(image)
    scores, row_stats, col_stats = scores_call(ip, iq, t)
    rows = reduce_rows(row_stats, pairs)
    cols = reduce_cols(col_stats)
    row_log = rows[0] + jnp.log(rows[1])
    col_log = cols[0] + jnp.log(cols[1])
    chunk = jnp.arange(16, dtype=jnp.int32)
    owner = (x * 2 + yl) * 32 + ((chunk // 2) * 2 + yh) * 2 + chunk % 2
    ids = owner[:, None] * CHUNK + jnp.arange(CHUNK, dtype=jnp.int32)[None, :]
    ids = ids.reshape(1, SIDE).astype(jnp.float32)
    g, gt, positive = logits_call(
        scores, ip, iq, row_log[None, :], col_log[None, :], rows[2][None, :], ids
    )
    grad_text = lax.psum_scatter(gt, ("z", "core"), scatter_dimension=0, tiled=True)
    grad_image = scatter_image(image_call(g, t))
    col_share = lax.dynamic_slice_in_dim(col_log, (z * 2 + core) * CHUNK, CHUNK, 0)
    loss = jnp.sum(row_log[:CHUNK]) + jnp.sum(col_share) - 2.0 * jnp.sum(positive)
    loss = jnp.full((8, 128), loss, jnp.float32)
    for step in (
        dict(dc=1), dict(dx=1), dict(dx=2), dict(dy=1), dict(dy=2), dict(dz=1), dict(dz=2), dict(dz=4)
    ):
        loss = loss + shift(loss, **step)
    return grad_image, grad_text, loss[0, 0] / (2.0 * CHUNK * 256)


def solution(mesh):
    shape = dict(mesh.shape)
    assert (shape["grp"], shape["mem"]) == (8, 32)
    grid = Mesh(mesh.devices.reshape(SIZES), AXES)
    by_mem = P(("z", "yh", "core", "x", "yl"))
    by_grp = P(AXES)
    rows = lambda spec: P(spec[0], None)
    return jax.shard_map(
        per_device,
        mesh=grid,
        in_specs=(rows(by_mem), rows(by_grp), by_mem),
        out_specs=(rows(by_mem), rows(by_grp), P()),
        check_vma=False,
    )
```

```python
import jax
import jax.numpy as jnp
import numpy as np
from jax import lax
from jax.experimental import pallas as pl
from jax.experimental.pallas import tpu as pltpu
from jax.sharding import Mesh, PartitionSpec as P

LOGIT_SCALE = 100.0
LN2 = float(np.log(2.0))
AXES = ("x", "yl", "z", "yh", "core")
SIZES = (4, 2, 8, 2, 2)
CHUNK = 80
WIDTH = 1280
HALF = WIDTH // 2
SIDE = 16 * CHUNK
COL_STEP = 256
MIB = 1024 * 1024
F32 = jnp.float32
BF16 = jnp.bfloat16


def moves(dx=0, dy=0, dz=0, dc=0, ring=0, line=0):
    out = []
    for x, yl, z, yh, c in np.ndindex(*SIZES):
        sx, sy = (line, ring) if c == 0 else (ring, line)
        y = (yh * 2 + yl + dy + sy) % 4
        to = ((x + dx + sx) % 4, y % 2, (z + dz) % 8, y // 2, (c + dc) % 2)
        out.append(
            (int(np.ravel_multi_index((x, yl, z, yh, c), SIZES)), int(np.ravel_multi_index(to, SIZES)))
        )
    return out


def shift(value, **step):
    return lax.ppermute(value, AXES, moves(**step))


def dot_t(a, b):
    return lax.dot_general(a, b, (((1,), (1,)), ((), ())), preferred_element_type=F32)


def lanes_of(block):
    pad = jnp.zeros((128 - CHUNK, 128), F32)
    return jnp.transpose(jnp.concatenate([block, pad], axis=0))


def columns_of(row):
    return jnp.transpose(jnp.broadcast_to(row, (128, 128)))[:CHUNK]


def rows_of(k):
    return pl.ds(pl.multiple_of(k * CHUNK, 16), CHUNK)


def scores_kernel(slots, text, mine_refs, swap_refs, pairs, ids, s_ref, i_ref, t_ref, row_ref, col_ref, peak, total, partner, csum, sems):
    core = slots[16]
    mine_cols = pl.ds(pl.multiple_of(core * HALF, 128), HALF)
    swap_cols = pl.ds(pl.multiple_of((1 - core) * HALF, 128), HALF)
    copies = []
    for z in range(8):
        for c in range(2):
            copies.append((text.at[pl.ds((z * 2 + c) * CHUNK, CHUNK)], t_ref.at[pl.ds((c * 8 + z) * CHUNK, CHUNK)]))
    for r in range(4):
        for l in range(4):
            copies.append((mine_refs[2 * r + l // 2].at[0, l % 2], i_ref.at[pl.ds((r * 4 + l) * CHUNK, CHUNK), mine_cols]))
            copies.append((swap_refs[r].at[l], i_ref.at[pl.ds((l * 4 + r) * CHUNK, CHUNK), swap_cols]))
    copies = [pltpu.make_async_copy(a, b, sems.at[n]) for n, (a, b) in enumerate(copies)]
    for copy in copies:
        copy.start()
    for k in range(16):
        partner[k * CHUNK : (k + 1) * CHUNK, :] = columns_of(pairs[pl.ds(slots[k], 1), :])
    csum[...] = jnp.zeros_like(csum)
    row_ref[2] = jnp.zeros((16, 128), F32)
    for copy in copies:
        copy.wait()

    def block(j, _):
        cols = pl.ds(pl.multiple_of(j * COL_STEP, COL_STEP), COL_STEP)
        s = (LOGIT_SCALE / LN2) * dot_t(i_ref[...], t_ref[cols, :])
        s_ref[:, cols] = s
        col_ref[0:1, cols] = jnp.max(s, axis=0, keepdims=True)
        lanes = s[:, :128]
        for k in range(1, COL_STEP // 128):
            lanes = jnp.maximum(lanes, s[:, k * 128 : (k + 1) * 128])

        @pl.when(j == 0)
        def _():
            peak[...] = lanes

        @pl.when(j > 0)
        def _():
            peak[...] = jnp.maximum(peak[...], lanes)

        return 0

    lax.fori_loop(0, SIDE // COL_STEP, block, 0)
    for k in range(16):
        rows = slice(k * CHUNK, (k + 1) * CHUNK)
        top = jnp.max(lanes_of(peak[rows, :]), axis=0, keepdims=True)
        row_ref[0, pl.ds(slots[k], 1), :] = top
        peak[rows, :] = columns_of(top)

    def sums(k, _):
        rows = rows_of(k)
        m = peak[rows, :]
        pair = partner[rows, :]
        acc = jnp.zeros((CHUNK, 128), F32)
        pos = jnp.zeros((CHUNK, 128), F32)
        for b in range(SIDE // 128):
            cols = slice(b * 128, (b + 1) * 128)
            s = s_ref[rows, cols]
            acc = acc + jnp.exp2(s - m)
            pos = pos + jnp.where(pair == ids[:, cols], s, 0.0)
            q = jnp.exp2(s - col_ref[0:1, cols])
            csum[:, cols] += jnp.sum(q.reshape(CHUNK // 8, 8, 128), axis=0)
        total[rows, :] = acc
        row_ref[2, 0:8, :] += jnp.sum(pos.reshape(CHUNK // 8, 8, 128), axis=0)
        return 0

    lax.fori_loop(0, 16, sums, 0)
    for k in range(16):
        rows = slice(k * CHUNK, (k + 1) * CHUNK)
        row_ref[1, pl.ds(slots[k], 1), :] = jnp.sum(lanes_of(total[rows, :]), axis=0, keepdims=True)
    col_ref[1:2, :] = jnp.sum(csum[...], axis=0, keepdims=True)


def text_grad(g_ref, i_ref, out_ref, start):
    for n in range(HALF // 128):
        cols = pl.ds(pl.multiple_of(start + n * 128, 128), 128)
        out = lax.dot_general(g_ref[:, cols], i_ref[...], (((0,), (0,)), ((), ())), preferred_element_type=F32)
        out_ref[n * 128 : (n + 1) * 128, :] = (LOGIT_SCALE * out).astype(BF16)


def logits_kernel(slots, s_ref, i_ref, row_log, col_log, pairs, ids, g_ref, out_ref, rows_log, partner):
    for k in range(16):
        rows = slice(k * CHUNK, (k + 1) * CHUNK)
        rows_log[rows, :] = columns_of(row_log[pl.ds(slots[k], 1), :]) + 1.0
        partner[rows, :] = columns_of(pairs[pl.ds(slots[k], 1), :])

    def block(k, _):
        rows = rows_of(k)
        r = rows_log[rows, :]
        pair = partner[rows, :]
        for b in range(SIDE // 128):
            cols = slice(b * 128, (b + 1) * 128)
            s = s_ref[rows, cols]
            g = jnp.exp2(s - r) + jnp.exp2(s - (col_log[:, cols] + 1.0))
            g_ref[rows, cols] = jnp.where(pair == ids[:, cols], g - 1.0, g).astype(BF16)
        return 0

    lax.fori_loop(0, 16, block, 0)
    text_grad(g_ref, i_ref, out_ref, (1 - slots[16]) * HALF)


def text_kernel(slots, g_ref, i_ref, out_ref):
    text_grad(g_ref, i_ref, out_ref, slots[16] * HALF)


def image_kernel(turn, slots, g_ref, t_ref, out_ref):
    half = slots[16] if turn == 0 else 1 - slots[16]
    t = t_ref[:, pl.ds(pl.multiple_of(half * HALF, 128), HALF)]

    def block(n, _):
        rows = pl.ds(pl.multiple_of(n * 256, 256), 256)
        out = jnp.dot(g_ref[rows, :], t, preferred_element_type=F32)
        out_ref[rows, :] = (LOGIT_SCALE * out).astype(BF16)
        return 0

    lax.fori_loop(0, SIDE // 256, block, 0)


FLOPS = 2 * SIDE * SIDE * WIDTH
VM = pl.BlockSpec(memory_space=pltpu.VMEM)
SM = pl.BlockSpec(memory_space=pltpu.SMEM)
AN = pl.BlockSpec(memory_space=pl.ANY)


def shaped(shape, dtype):
    return jax.ShapeDtypeStruct(shape, dtype)


def cost(flops, byts, exps=0):
    return pl.CostEstimate(flops=int(flops), bytes_accessed=int(byts), transcendentals=int(exps))


def params(mib):
    return pltpu.CompilerParams(vmem_limit_bytes=mib * MIB)


def scores_call(slots, text, mine, swap, pairs, ids):
    return pl.pallas_call(
        scores_kernel,
        out_shape=(
            shaped((SIDE, SIDE), F32),
            shaped((SIDE, WIDTH), BF16),
            shaped((SIDE, WIDTH), BF16),
            shaped((3, 16, 128), F32),
            shaped((2, SIDE), F32),
        ),
        in_specs=[SM, AN, [AN] * 8, [AN] * 4, VM, VM],
        out_specs=(VM,) * 5,
        scratch_shapes=[pltpu.VMEM((SIDE, 128), F32)] * 3 + [pltpu.VMEM((8, SIDE), F32), pltpu.SemaphoreType.DMA((48,))],
        cost_estimate=cost(FLOPS, 18 * MIB, 2 * SIDE * SIDE),
        compiler_params=params(28),
    )(slots, text, mine, swap, pairs, ids)


def logits_call(slots, s, i, row_log, col_log, pairs, ids):
    return pl.pallas_call(
        logits_kernel,
        out_shape=(shaped((SIDE, SIDE), BF16), shaped((HALF, WIDTH), BF16)),
        in_specs=[SM] + [VM] * 6,
        out_specs=(VM, VM),
        scratch_shapes=[pltpu.VMEM((SIDE, 128), F32)] * 2,
        cost_estimate=cost(FLOPS // 2, 16 * MIB, 2 * SIDE * SIDE),
        compiler_params=params(28),
    )(slots, s, i, row_log, col_log, pairs, ids)


def text_call(slots, g, i):
    return pl.pallas_call(
        text_kernel,
        out_shape=shaped((HALF, WIDTH), BF16),
        in_specs=[SM, VM, VM],
        out_specs=VM,
        cost_estimate=cost(FLOPS // 2, 8 * MIB),
        compiler_params=params(20),
    )(slots, g, i)


def image_call(turn, slots, g, t):
    return pl.pallas_call(
        lambda *refs: image_kernel(turn, *refs),
        out_shape=shaped((SIDE, HALF), BF16),
        in_specs=[SM, VM, VM],
        out_specs=VM,
        cost_estimate=cost(FLOPS // 2, 8 * MIB),
        compiler_params=params(20),
    )(slots, g, t)


def pick(core, first, second):
    return jnp.where(core == 0, first, second)


def gather_image(core, image):
    left, right = image[:, :HALF], image[:, HALF:]
    other = shift(pick(core, right, left), dc=1)
    own = jnp.stack([pick(core, left, right), other])[:, None]
    l1, l3, l2 = shift(own, line=1), shift(own, line=-1), shift(own, line=2)
    a, b = jnp.concatenate([own, l1], axis=1), jnp.concatenate([l2, l3], axis=1)
    a1, b3 = shift(a, ring=1), shift(b, ring=-1)
    b1, a3 = shift(b, ring=1), shift(a, ring=-1)
    a2, b2 = shift(a1, ring=1), shift(b3, ring=-1)
    blocks = [(a, b), (a1, b1), (a2, b2), (a3, b3)]
    swap = [shift(jnp.concatenate([p[1], q[1]], axis=0), dc=1) for p, q in blocks]
    return [piece for block in blocks for piece in block], swap


def scatter_image(core, own, other):
    own = own.reshape(4, 4, CHUNK, HALF)
    other = jnp.swapaxes(other.reshape(4, 4, CHUNK, HALF), 0, 1)
    part = lambda r, l: jnp.stack([own[r, l : l + 2], other[r, l : l + 2]])
    a2 = shift(part(2, 0), ring=-1)
    b2 = shift(part(2, 2), ring=1)
    b1 = shift(part(1, 2), ring=-1)
    a3 = shift(part(3, 0), ring=1)
    a1 = shift((part(1, 0).astype(F32) + a2.astype(F32)).astype(BF16), ring=-1)
    b3 = shift((part(3, 2).astype(F32) + b2.astype(F32)).astype(BF16), ring=1)
    a = part(0, 0).astype(F32) + a1.astype(F32) + a3.astype(F32)
    b = part(0, 2).astype(F32) + b1.astype(F32) + b3.astype(F32)
    from_up = shift(a[:, 1].astype(BF16), line=-1)
    from_far = shift(b[:, 0].astype(BF16), line=2)
    from_down = shift(b[:, 1].astype(BF16), line=1)
    sums = a[:, 0] + from_up.astype(F32) + from_far.astype(F32) + from_down.astype(F32)
    sums = sums.astype(BF16)
    swapped = shift(sums[1], dc=1)
    return pick(core, jnp.concatenate([sums[0], swapped], axis=1), jnp.concatenate([swapped, sums[0]], axis=1))


def merge(one, two):
    top = jnp.maximum(one[0], two[0])
    return top, one[1] * jnp.exp2(one[0] - top) + two[1] * jnp.exp2(two[0] - top)


XY_ROUNDS = (dict(dx=1), dict(dx=2), dict(dy=1), dict(dy=2))
Z_ROUNDS = (dict(dc=1), dict(dz=1), dict(dz=2), dict(dz=4))


def per_device(image, text, pairs):
    x, yl, z, yh, core = (lax.axis_index(name).astype(jnp.int32) for name in AXES)
    y = yh * 2 + yl
    texts = lax.all_gather(text, ("z", "core"), axis=0, tiled=True)
    mine, swap = gather_image(core, image)

    steps = jnp.arange(16, dtype=jnp.int32)
    ring, line = steps // 4, steps % 4
    slots = pick(core, ((x - line) % 4) * 4 + (y - ring) % 4, ((x - ring) % 4) * 4 + (y - line) % 4)
    slots = jnp.concatenate([slots, core[None]])
    known = jnp.pad(pairs.astype(F32), (0, 128 - CHUNK), constant_values=-1.0)
    known = jnp.where(steps[:, None] == x * 4 + y, known[None, :], -1.0)
    for step in XY_ROUNDS:
        known = jnp.maximum(known, shift(known, **step))
    owner = (x * 2 + yl) * 32 + ((steps % 8) * 2 + yh) * 2 + steps // 8
    ids = owner[:, None] * CHUNK + jnp.arange(CHUNK, dtype=jnp.int32)[None, :]
    ids = ids.reshape(1, SIDE).astype(F32)

    scores, rows, cols, row_stats, col_stats = scores_call(slots, texts, mine, swap, known, ids)
    for step in XY_ROUNDS:
        other = shift(row_stats, **step)
        row_stats = jnp.stack([*merge(row_stats, other), row_stats[2] + other[2]])
    for step in Z_ROUNDS:
        col_stats = jnp.stack(merge(col_stats, shift(col_stats, **step)))
    row_log = row_stats[0] + jnp.log2(row_stats[1])
    col_log = col_stats[0] + jnp.log2(col_stats[1])

    in_rows = (jnp.arange(128) < CHUNK)[None, :]
    row_loss = jnp.sum(jnp.where(in_rows, row_log, 0.0)) - 2.0 * jnp.sum(row_stats[2])
    row_loss = jnp.full((8, 128), row_loss, F32)
    col_loss = jnp.full((8, 128), jnp.sum(col_log), F32)
    for z_step, xy_step in zip(Z_ROUNDS, XY_ROUNDS):
        row_loss = row_loss + shift(row_loss, **z_step)
        col_loss = col_loss + shift(col_loss, **xy_step)
    loss = (LN2 / (2.0 * 256 * CHUNK)) * (row_loss + col_loss)[0, 0]

    g, text_other = logits_call(slots, scores, rows, row_log, col_log[None, :], known, ids)
    text_swapped = shift(text_other, dc=1)
    text_own = text_call(slots, g, rows)
    text_sum = (text_own.astype(F32) + text_swapped.astype(F32)).astype(BF16)
    grad_text = lax.psum_scatter(text_sum, "z", scatter_dimension=0, tiled=True)
    image_other = shift(image_call(1, slots, g, cols), dc=1)
    image_own = image_call(0, slots, g, cols)
    grad_image = scatter_image(core, image_own, image_other)
    return grad_image, grad_text, loss


def solution(mesh):
    shape = dict(mesh.shape)
    assert (shape["grp"], shape["mem"]) == (8, 32)
    grid = Mesh(mesh.devices.reshape(SIZES), AXES)
    by_mem = ("z", "yh", "core", "x", "yl")
    return jax.shard_map(
        per_device,
        mesh=grid,
        in_specs=(P(by_mem, None), P(AXES, None), P(by_mem)),
        out_specs=(P(by_mem, None), P(AXES, None), P()),
        check_vma=False,
    )
```

```python
import jax
import jax.numpy as jnp
import numpy as np
from jax import lax
from jax.experimental import pallas as pl
from jax.experimental.pallas import tpu as pltpu
from jax.sharding import Mesh, PartitionSpec as P

LOGIT_SCALE = 100.0
LN2 = float(np.log(2.0))
AXES = ("x", "yl", "z", "yh", "core")
SIZES = (4, 2, 8, 2, 2)
CHUNK = 80
WIDTH = 1280
HALF = WIDTH // 2
SIDE = 16 * CHUNK
COL_STEP = 256
MIB = 1024 * 1024
F32 = jnp.float32
BF16 = jnp.bfloat16


def moves(dx=0, dy=0, dz=0, dc=0, ring=0, line=0):
    out = []
    for x, yl, z, yh, c in np.ndindex(*SIZES):
        sx, sy = (line, ring) if c == 0 else (ring, line)
        y = (yh * 2 + yl + dy + sy) % 4
        to = ((x + dx + sx) % 4, y % 2, (z + dz) % 8, y // 2, (c + dc) % 2)
        out.append(
            (int(np.ravel_multi_index((x, yl, z, yh, c), SIZES)), int(np.ravel_multi_index(to, SIZES)))
        )
    return out


def shift(value, **step):
    return lax.ppermute(value, AXES, moves(**step))


def after(value, *done):
    return lax.optimization_barrier((value, *done))[0]


def dot_t(a, b):
    return lax.dot_general(a, b, (((1,), (1,)), ((), ())), preferred_element_type=F32)


def lanes_of(block):
    pad = jnp.zeros((128 - CHUNK, 128), F32)
    return jnp.transpose(jnp.concatenate([block, pad], axis=0))


def columns_of(row):
    return jnp.transpose(jnp.broadcast_to(row, (128, 128)))[:CHUNK]


def rows_of(k):
    return pl.ds(pl.multiple_of(k * CHUNK, 16), CHUNK)


def chunk_of(blocks, ring, line):
    if ring == 2:
        return blocks[2 + line // 2][line % 2]
    return blocks[{0: 0, 1: 1, 3: 4}[ring]][line]


def scores_kernel(slots, text, mine, swap, pairs, ids, s_ref, i_ref, t_ref, row_ref, col_ref, peak, total, partner, csum):
    core = slots[16]
    mine_cols = pl.ds(pl.multiple_of(core * HALF, 128), HALF)
    swap_cols = pl.ds(pl.multiple_of((1 - core) * HALF, 128), HALF)
    for z in range(8):
        for c in range(2):
            t_ref[(c * 8 + z) * CHUNK : (c * 8 + z + 1) * CHUNK, :] = text[(z * 2 + c) * CHUNK : (z * 2 + c + 1) * CHUNK, :]
    for r in range(4):
        for l in range(4):
            rows = slice((r * 4 + l) * CHUNK, (r * 4 + l + 1) * CHUNK)
            i_ref[rows, mine_cols] = chunk_of(mine, r, l)[0]
            i_ref[rows, swap_cols] = chunk_of(swap, l, r)[1]
    for k in range(16):
        partner[k * CHUNK : (k + 1) * CHUNK, :] = columns_of(pairs[pl.ds(slots[k], 1), :])
    csum[...] = jnp.zeros_like(csum)
    row_ref[2] = jnp.zeros((16, 128), F32)

    def block(j, _):
        cols = pl.ds(pl.multiple_of(j * COL_STEP, COL_STEP), COL_STEP)
        s = (LOGIT_SCALE / LN2) * dot_t(i_ref[...], t_ref[cols, :])
        s_ref[:, cols] = s
        col_ref[0:1, cols] = jnp.max(s, axis=0, keepdims=True)
        lanes = s[:, :128]
        for k in range(1, COL_STEP // 128):
            lanes = jnp.maximum(lanes, s[:, k * 128 : (k + 1) * 128])

        @pl.when(j == 0)
        def _():
            peak[...] = lanes

        @pl.when(j > 0)
        def _():
            peak[...] = jnp.maximum(peak[...], lanes)

        return 0

    lax.fori_loop(0, SIDE // COL_STEP, block, 0)
    for k in range(16):
        rows = slice(k * CHUNK, (k + 1) * CHUNK)
        top = jnp.max(lanes_of(peak[rows, :]), axis=0, keepdims=True)
        row_ref[0, pl.ds(slots[k], 1), :] = top
        peak[rows, :] = columns_of(top)

    def sums(k, _):
        rows = rows_of(k)
        m = peak[rows, :]
        pair = partner[rows, :]
        acc = jnp.zeros((CHUNK, 128), F32)
        pos = jnp.zeros((CHUNK, 128), F32)
        for b in range(SIDE // 128):
            cols = slice(b * 128, (b + 1) * 128)
            s = s_ref[rows, cols]
            acc = acc + jnp.exp2(s - m)
            pos = pos + jnp.where(pair == ids[:, cols], s, 0.0)
            q = jnp.exp2(s - col_ref[0:1, cols])
            csum[:, cols] += jnp.sum(q.reshape(CHUNK // 8, 8, 128), axis=0)
        total[rows, :] = acc
        row_ref[2, 0:8, :] += jnp.sum(pos.reshape(CHUNK // 8, 8, 128), axis=0)
        return 0

    lax.fori_loop(0, 16, sums, 0)
    for k in range(16):
        rows = slice(k * CHUNK, (k + 1) * CHUNK)
        row_ref[1, pl.ds(slots[k], 1), :] = jnp.sum(lanes_of(total[rows, :]), axis=0, keepdims=True)
    col_ref[1:2, :] = jnp.sum(csum[...], axis=0, keepdims=True)


def text_grad(g_ref, i_ref, out_ref, start, add_ref=None):
    for n in range(HALF // 128):
        cols = pl.ds(pl.multiple_of(start + n * 128, 128), 128)
        rows = slice(n * 128, (n + 1) * 128)
        out = lax.dot_general(g_ref[:, cols], i_ref[...], (((0,), (0,)), ((), ())), preferred_element_type=F32)
        out = LOGIT_SCALE * out
        if add_ref is not None:
            out = out + add_ref[rows, :].astype(F32)
        out_ref[rows, :] = out.astype(BF16)


def logits_kernel(slots, s_ref, row_ref, col_ref, pairs, ids, t_ref, g_ref, out_ref, loss_ref, logs, rows_log, partner):
    logs[...] = row_ref[0] + jnp.log2(row_ref[1])
    col_log = col_ref[0:1, :] + jnp.log2(col_ref[1:2, :])
    kept = lax.broadcasted_iota(jnp.int32, (16, 128), 1) < CHUNK
    kept = jnp.where(kept, logs[...], 0.0) - 2.0 * row_ref[2]
    loss_ref[0] = kept[:8] + kept[8:]
    tail = col_log[:, :128]
    for b in range(1, SIDE // 128):
        tail = tail + col_log[:, b * 128 : (b + 1) * 128]
    loss_ref[1] = jnp.concatenate([tail, jnp.zeros((7, 128), F32)], axis=0)
    col_log = col_log + 1.0
    for k in range(16):
        rows = slice(k * CHUNK, (k + 1) * CHUNK)
        rows_log[rows, :] = columns_of(logs[pl.ds(slots[k], 1), :]) + 1.0
        partner[rows, :] = columns_of(pairs[pl.ds(slots[k], 1), :])

    def block(k, _):
        rows = rows_of(k)
        r = rows_log[rows, :]
        pair = partner[rows, :]
        for b in range(SIDE // 128):
            cols = slice(b * 128, (b + 1) * 128)
            s = s_ref[rows, cols]
            g = jnp.exp2(s - r) + jnp.exp2(s - col_log[:, cols])
            g_ref[rows, cols] = jnp.where(pair == ids[:, cols], g - 1.0, g).astype(BF16)
        return 0

    lax.fori_loop(0, 16, block, 0)
    t = half_of(t_ref, 1 - slots[16])
    for r in range(4):
        rows = slice(r * 4 * CHUNK, (r + 1) * 4 * CHUNK)
        out = jnp.dot(g_ref[rows, :], t, preferred_element_type=F32)
        out_ref[rows, :] = (LOGIT_SCALE * out).astype(BF16)


def text_other_kernel(slots, g_ref, i_ref, out_ref):
    text_grad(g_ref, i_ref, out_ref, (1 - slots[16]) * HALF)


def text_own_kernel(slots, g_ref, i_ref, add_ref, out_ref):
    text_grad(g_ref, i_ref, out_ref, slots[16] * HALF, add_ref)


def half_of(t_ref, half):
    return t_ref[:, pl.ds(pl.multiple_of(half * HALF, 128), HALF)]


def image_kernel(rings, slots, g_ref, t_ref, swap_ref, *outs):
    t = half_of(t_ref, slots[16])
    for n, r in enumerate(rings):
        out = jnp.dot(g_ref[r * 4 * CHUNK : (r + 1) * 4 * CHUNK, :], t, preferred_element_type=F32)
        out = (LOGIT_SCALE * out).astype(BF16)
        for l in range(4):
            ref, place = (outs[l // 2], l % 2) if r == 2 else (outs[n], l)
            ref[place, 0] = out[l * CHUNK : (l + 1) * CHUNK]
            ref[place, 1] = swap_ref[(l * 4 + r) * CHUNK : (l * 4 + r + 1) * CHUNK, :]


FLOPS = 2 * SIDE * SIDE * WIDTH
VM = pl.BlockSpec(memory_space=pltpu.VMEM)
SM = pl.BlockSpec(memory_space=pltpu.SMEM)


def shaped(shape, dtype):
    return jax.ShapeDtypeStruct(shape, dtype)


def cost(flops, byts, exps=0):
    return pl.CostEstimate(flops=int(flops), bytes_accessed=int(byts), transcendentals=int(exps))


def params(mib):
    return pltpu.CompilerParams(vmem_limit_bytes=mib * MIB)


def scores_call(slots, text, mine, swap, pairs, ids):
    return pl.pallas_call(
        scores_kernel,
        out_shape=(
            shaped((SIDE, SIDE), F32),
            shaped((SIDE, WIDTH), BF16),
            shaped((SIDE, WIDTH), BF16),
            shaped((3, 16, 128), F32),
            shaped((2, SIDE), F32),
        ),
        in_specs=[SM, VM, [VM] * 5, [VM] * 5, VM, VM],
        out_specs=(VM,) * 5,
        scratch_shapes=[pltpu.VMEM((SIDE, 128), F32)] * 3 + [pltpu.VMEM((8, SIDE), F32)],
        cost_estimate=cost(FLOPS, 18 * MIB, 2 * SIDE * SIDE),
        compiler_params=params(28),
    )(slots, text, mine, swap, pairs, ids)


def logits_call(slots, s, row_stats, col_stats, pairs, ids, t):
    return pl.pallas_call(
        logits_kernel,
        out_shape=(shaped((SIDE, SIDE), BF16), shaped((SIDE, HALF), BF16), shaped((2, 8, 128), F32)),
        in_specs=[SM] + [VM] * 6,
        out_specs=(VM, VM, VM),
        scratch_shapes=[pltpu.VMEM((16, 128), F32)] + [pltpu.VMEM((SIDE, 128), F32)] * 2,
        cost_estimate=cost(FLOPS // 2, 16 * MIB, 2 * SIDE * SIDE),
        compiler_params=params(28),
    )(slots, s, row_stats, col_stats, pairs, ids, t)


def text_call(slots, g, i, add=None):
    return pl.pallas_call(
        text_other_kernel if add is None else text_own_kernel,
        out_shape=shaped((HALF, WIDTH), BF16),
        in_specs=[SM] + [VM] * (2 if add is None else 3),
        out_specs=VM,
        cost_estimate=cost(FLOPS // 2, 10 * MIB),
        compiler_params=params(20),
    )(*((slots, g, i) if add is None else (slots, g, i, add)))


def image_call(rings, slots, g, t, swapped):
    shapes = [(2, 2, CHUNK, HALF)] * 2 if rings == (2,) else [(4, 2, CHUNK, HALF)] * len(rings)
    return pl.pallas_call(
        lambda *refs: image_kernel(rings, *refs),
        out_shape=tuple(shaped(shape, BF16) for shape in shapes),
        in_specs=[SM, VM, VM, VM],
        out_specs=(VM,) * len(shapes),
        cost_estimate=cost(FLOPS // 8 * len(rings), 10 * MIB),
        compiler_params=params(20),
    )(slots, g, t, swapped)


def pick(core, first, second):
    return jnp.where(core == 0, first, second)


def gather_image(core, image, known):
    left, right = image[:, :HALF], image[:, HALF:]
    other = shift(pick(core, right, left), dc=1)
    own = jnp.stack([pick(core, left, right), other])[None]
    l1, l3, l2 = shift(own, line=1), shift(own, line=-1), shift(own, line=2)
    known = jnp.maximum(known, shift(known, line=1))
    l1, l2, l3, known = lax.optimization_barrier((l1, l2, l3, known))
    block = jnp.concatenate([own, l1, l2, l3], axis=0)
    up, down = shift(block, ring=1), shift(block, ring=-1)
    known = jnp.maximum(known, shift(known, line=2))
    known = jnp.maximum(known, shift(known, ring=1))
    up, down, known = lax.optimization_barrier((up, down, known))
    a, b = shift(up[:2], ring=1), shift(down[2:], ring=-1)
    known = jnp.maximum(known, shift(known, ring=2))
    a, b, known = lax.optimization_barrier((a, b, known))
    mine = [block, up, a, b, down]
    return mine, [shift(piece, dc=1) for piece in mine], known


def loss_round(n, losses):
    return [losses[0] + shift(losses[0], **Z_ROUNDS[n]), losses[1] + shift(losses[1], **XY_ROUNDS[n])]


def add_lines(block, line, part):
    total = block[line : line + 2].astype(F32) + part.astype(F32)
    return lax.dynamic_update_slice(block, total.astype(BF16), (line, 0, 0, 0))


def merge(one, two):
    top = jnp.maximum(one[0], two[0])
    return top, one[1] * jnp.exp2(one[0] - top) + two[1] * jnp.exp2(two[0] - top)


XY_ROUNDS = (dict(dx=1), dict(dx=2), dict(dy=1), dict(dy=2))
Z_ROUNDS = (dict(dc=1), dict(dz=1), dict(dz=2), dict(dz=4))


def per_device(image, text, pairs):
    x, yl, z, yh, core = (lax.axis_index(name).astype(jnp.int32) for name in AXES)
    y = yh * 2 + yl
    texts = lax.all_gather(text, ("z", "core"), axis=0, tiled=True)

    steps = jnp.arange(16, dtype=jnp.int32)
    ring, line = steps // 4, steps % 4
    slots = pick(core, ((x - line) % 4) * 4 + (y - ring) % 4, ((x - ring) % 4) * 4 + (y - line) % 4)
    slots = jnp.concatenate([slots, core[None]])
    known = jnp.pad(pairs.astype(F32), (0, 128 - CHUNK), constant_values=-1.0)
    known = jnp.where(steps[:, None] == x * 4 + y, known[None, :], -1.0)
    mine, swap, known = gather_image(core, image, known)
    owner = (x * 2 + yl) * 32 + ((steps % 8) * 2 + yh) * 2 + steps // 8
    ids = owner[:, None] * CHUNK + jnp.arange(CHUNK, dtype=jnp.int32)[None, :]
    ids = ids.reshape(1, SIDE).astype(F32)

    scores, rows, cols, row_stats, col_stats = scores_call(slots, texts, mine, swap, known, ids)
    for step in XY_ROUNDS:
        other = shift(row_stats, **step)
        row_stats = jnp.stack([*merge(row_stats, other), row_stats[2] + other[2]])
    for step in Z_ROUNDS:
        col_stats = jnp.stack(merge(col_stats, shift(col_stats, **step)))
    g, image_other, losses = logits_call(slots, scores, row_stats, col_stats, known, ids, cols)
    image_swapped = shift(image_other, dc=1)
    text_other = text_call(slots, g, rows)
    text_swapped = shift(text_other, dc=1)
    a2, b2 = image_call((2,), slots, after(g, text_other), cols, image_swapped)
    text_sum = text_call(slots, after(g, a2), rows, text_swapped)
    grad_text = lax.psum_scatter(text_sum, "z", scatter_dimension=0, tiled=True)
    down, up = image_call((1, 3), slots, after(g, text_sum), cols, image_swapped)
    a2, b2 = shift(a2, ring=-1), shift(b2, ring=1)
    losses = loss_round(0, (after(losses[0], down), after(losses[1], down)))
    a2, b2, *losses = lax.optimization_barrier((a2, b2, *losses))
    down = shift(add_lines(down, 0, a2), ring=-1)
    up = shift(add_lines(up, 2, b2), ring=1)
    (rest,) = image_call((0,), slots, after(g, a2), cols, image_swapped)
    losses = loss_round(2, loss_round(1, losses))
    down, up, *losses = lax.optimization_barrier((down, up, *losses))
    sums = rest.astype(F32) + down.astype(F32) + up.astype(F32)
    from_up = shift(sums[1].astype(BF16), line=-1)
    from_down = shift(sums[3].astype(BF16), line=1)
    from_far = shift(sums[2].astype(BF16), line=2)
    losses = loss_round(3, losses)
    from_up, from_down, from_far, *losses = lax.optimization_barrier((from_up, from_down, from_far, *losses))
    sums = sums[0] + from_up.astype(F32) + from_far.astype(F32) + from_down.astype(F32)
    sums = sums.astype(BF16)
    swapped = shift(sums[1], dc=1)
    grad_image = pick(
        core, jnp.concatenate([sums[0], swapped], axis=1), jnp.concatenate([swapped, sums[0]], axis=1)
    )
    loss = (LN2 / (2.0 * 256 * CHUNK)) * jnp.sum(losses[0] + losses[1])
    return grad_image, grad_text, loss


def solution(mesh):
    shape = dict(mesh.shape)
    assert (shape["grp"], shape["mem"]) == (8, 32)
    grid = Mesh(mesh.devices.reshape(SIZES), AXES)
    by_mem = ("z", "yh", "core", "x", "yl")
    return jax.shard_map(
        per_device,
        mesh=grid,
        in_specs=(P(by_mem, None), P(AXES, None), P(by_mem)),
        out_specs=(P(by_mem, None), P(AXES, None), P()),
        check_vma=False,
    )
```

```python
import jax
import jax.numpy as jnp
import numpy as np
from jax import lax
from jax.experimental import pallas as pl
from jax.experimental.pallas import tpu as pltpu
from jax.sharding import Mesh, PartitionSpec as P

LOGIT_SCALE = 100.0
LN2 = float(np.log(2.0))
AXES = ("x", "yl", "z", "yh", "core")
SIZES = (4, 2, 8, 2, 2)
CHUNK = 80
WIDTH = 1280
HALF = WIDTH // 2
SIDE = 16 * CHUNK
COL_STEP = 256
MIB = 1024 * 1024
F32 = jnp.float32
BF16 = jnp.bfloat16


def moves(dx=0, dy=0, dz=0, dc=0, ring=0, line=0, fork=0):
    out = []
    for x, yl, z, yh, c in np.ndindex(*SIZES):
        sx, sy = (line, ring) if c == 0 else (ring, line)
        y = (yh * 2 + yl + dy + sy) % 4
        to = ((x + dx + sx) % 4, y % 2, (z + dz + (fork if c == 0 else -fork)) % 8, y // 2, (c + dc) % 2)
        out.append(
            (int(np.ravel_multi_index((x, yl, z, yh, c), SIZES)), int(np.ravel_multi_index(to, SIZES)))
        )
    return out


def shift(value, **step):
    return lax.ppermute(value, AXES, moves(**step))


def after(value, *done):
    return lax.optimization_barrier((value, *done))[0]


def dot_t(a, b):
    return lax.dot_general(a, b, (((1,), (1,)), ((), ())), preferred_element_type=F32)


def lanes_of(block):
    pad = jnp.zeros((128 - CHUNK, 128), F32)
    return jnp.transpose(jnp.concatenate([block, pad], axis=0))


def columns_of(row):
    return jnp.transpose(jnp.broadcast_to(row, (128, 128)))[:CHUNK]


def rows_of(k):
    return pl.ds(pl.multiple_of(k * CHUNK, 16), CHUNK)


def chunk_of(blocks, ring, line):
    if ring == 2:
        return blocks[2 + line // 2][line % 2]
    return blocks[{0: 0, 1: 1, 3: 4}[ring]][line]


def scores_kernel(slots, text, mine, swap, pairs, ids, s_ref, i_ref, t_ref, row_ref, col_ref, peak, total, partner, csum):
    core = slots[16]
    mine_cols = pl.ds(pl.multiple_of(core * HALF, 128), HALF)
    swap_cols = pl.ds(pl.multiple_of((1 - core) * HALF, 128), HALF)
    for z in range(8):
        for c in range(2):
            t_ref[(c * 8 + z) * CHUNK : (c * 8 + z + 1) * CHUNK, :] = text[(z * 2 + c) * CHUNK : (z * 2 + c + 1) * CHUNK, :]
    for r in range(4):
        for l in range(4):
            rows = slice((r * 4 + l) * CHUNK, (r * 4 + l + 1) * CHUNK)
            i_ref[rows, mine_cols] = chunk_of(mine, r, l)[0]
            i_ref[rows, swap_cols] = chunk_of(swap, l, r)[1]
    for k in range(16):
        partner[k * CHUNK : (k + 1) * CHUNK, :] = columns_of(pairs[pl.ds(slots[k], 1), :])
    row_ref[2] = jnp.zeros((16, 128), F32)

    for j in range(SIDE // COL_STEP + 1):
        if j < SIDE // COL_STEP:
            cols = slice(j * COL_STEP, (j + 1) * COL_STEP)
            s = (LOGIT_SCALE / LN2) * dot_t(i_ref[...], t_ref[cols, :])
            s_ref[:, cols] = s
            col_ref[0:1, cols] = jnp.max(s, axis=0, keepdims=True)
            lanes = jnp.maximum(s[:, :128], s[:, 128:])
            peak[...] = lanes if j == 0 else jnp.maximum(peak[...], lanes)
        if j > 0:
            cols = slice((j - 1) * COL_STEP, j * COL_STEP)
            q = jnp.exp2(s_ref[:, cols] - col_ref[0:1, cols])
            col_ref[1:2, cols] = jnp.sum(q, axis=0, keepdims=True)
    for k in range(16):
        rows = slice(k * CHUNK, (k + 1) * CHUNK)
        top = jnp.max(lanes_of(peak[rows, :]), axis=0, keepdims=True)
        row_ref[0, pl.ds(slots[k], 1), :] = top
        peak[rows, :] = columns_of(top)

    def sums(k, _):
        rows = rows_of(k)
        m = peak[rows, :]
        pair = partner[rows, :]
        acc = jnp.zeros((CHUNK, 128), F32)
        pos = jnp.zeros((CHUNK, 128), F32)
        for b in range(SIDE // 128):
            cols = slice(b * 128, (b + 1) * 128)
            s = s_ref[rows, cols]
            acc = acc + jnp.exp2(s - m)
            pos = pos + jnp.where(pair == ids[:, cols], s, 0.0)
        total[rows, :] = acc
        row_ref[2, 0:8, :] += jnp.sum(pos.reshape(CHUNK // 8, 8, 128), axis=0)
        return 0

    lax.fori_loop(0, 16, sums, 0)
    for k in range(16):
        rows = slice(k * CHUNK, (k + 1) * CHUNK)
        row_ref[1, pl.ds(slots[k], 1), :] = jnp.sum(lanes_of(total[rows, :]), axis=0, keepdims=True)


def text_grad(g_ref, i_ref, out_ref, start, add_ref=None):
    for n in range(HALF // 128):
        cols = pl.ds(pl.multiple_of(start + n * 128, 128), 128)
        rows = slice(n * 128, (n + 1) * 128)
        out = lax.dot_general(g_ref[:, cols], i_ref[...], (((0,), (0,)), ((), ())), preferred_element_type=F32)
        out = LOGIT_SCALE * out
        if add_ref is not None:
            out = out + add_ref[rows, :].astype(F32)
        out_ref[rows, :] = out.astype(BF16)


def logits_kernel(slots, s_ref, row_ref, col_ref, pairs, ids, t_ref, g_ref, out_ref, loss_ref, logs, rows_log, partner):
    logs[...] = row_ref[0] + jnp.log2(row_ref[1])
    col_log = col_ref[0:1, :] + jnp.log2(col_ref[1:2, :])
    kept = lax.broadcasted_iota(jnp.int32, (16, 128), 1) < CHUNK
    kept = jnp.where(kept, logs[...], 0.0) - 2.0 * row_ref[2]
    loss_ref[0] = kept[:8] + kept[8:]
    tail = col_log[:, :128]
    for b in range(1, SIDE // 128):
        tail = tail + col_log[:, b * 128 : (b + 1) * 128]
    loss_ref[1] = jnp.concatenate([tail, jnp.zeros((7, 128), F32)], axis=0)
    col_log = col_log + 1.0
    for k in range(16):
        rows = slice(k * CHUNK, (k + 1) * CHUNK)
        rows_log[rows, :] = columns_of(logs[pl.ds(slots[k], 1), :]) + 1.0
        partner[rows, :] = columns_of(pairs[pl.ds(slots[k], 1), :])

    def block(k, _):
        rows = rows_of(k)
        r = rows_log[rows, :]
        pair = partner[rows, :]
        for b in range(SIDE // 128):
            cols = slice(b * 128, (b + 1) * 128)
            s = s_ref[rows, cols]
            g = jnp.exp2(s - r) + jnp.exp2(s - col_log[:, cols])
            g_ref[rows, cols] = jnp.where(pair == ids[:, cols], g - 1.0, g).astype(BF16)
        return 0

    lax.fori_loop(0, 16, block, 0)
    t = half_of(t_ref, 1 - slots[16])
    for r in range(4):
        rows = slice(r * 4 * CHUNK, (r + 1) * 4 * CHUNK)
        out = jnp.dot(g_ref[rows, :], t, preferred_element_type=F32)
        out_ref[rows, :] = (LOGIT_SCALE * out).astype(BF16)


def text_other_kernel(slots, g_ref, i_ref, out_ref):
    text_grad(g_ref, i_ref, out_ref, (1 - slots[16]) * HALF)


def text_own_kernel(slots, g_ref, i_ref, add_ref, out_ref):
    text_grad(g_ref, i_ref, out_ref, slots[16] * HALF, add_ref)


def half_of(t_ref, half):
    return t_ref[:, pl.ds(pl.multiple_of(half * HALF, 128), HALF)]


def image_kernel(rings, slots, g_ref, t_ref, swap_ref, *outs):
    t = half_of(t_ref, slots[16])
    for n, r in enumerate(rings):
        out = jnp.dot(g_ref[r * 4 * CHUNK : (r + 1) * 4 * CHUNK, :], t, preferred_element_type=F32)
        out = (LOGIT_SCALE * out).astype(BF16)
        for l in range(4):
            ref, place = (outs[l // 2], l % 2) if r == 2 else (outs[n], l)
            ref[place, 0] = out[l * CHUNK : (l + 1) * CHUNK]
            ref[place, 1] = swap_ref[(l * 4 + r) * CHUNK : (l * 4 + r + 1) * CHUNK, :]


FLOPS = 2 * SIDE * SIDE * WIDTH
VM = pl.BlockSpec(memory_space=pltpu.VMEM)
SM = pl.BlockSpec(memory_space=pltpu.SMEM)


def shaped(shape, dtype):
    return jax.ShapeDtypeStruct(shape, dtype)


def cost(flops, byts, exps=0):
    return pl.CostEstimate(flops=1000, bytes_accessed=1000, transcendentals=0)


def params(mib):
    return pltpu.CompilerParams(vmem_limit_bytes=mib * MIB)


def scores_call(slots, text, mine, swap, pairs, ids):
    return pl.pallas_call(
        scores_kernel,
        out_shape=(
            shaped((SIDE, SIDE), F32),
            shaped((SIDE, WIDTH), BF16),
            shaped((SIDE, WIDTH), BF16),
            shaped((3, 16, 128), F32),
            shaped((2, SIDE), F32),
        ),
        in_specs=[SM, VM, [VM] * 5, [VM] * 5, VM, VM],
        out_specs=(VM,) * 5,
        scratch_shapes=[pltpu.VMEM((SIDE, 128), F32)] * 3 + [pltpu.VMEM((8, SIDE), F32)],
        cost_estimate=cost(FLOPS, 18 * MIB, 2 * SIDE * SIDE),
        compiler_params=params(28),
    )(slots, text, mine, swap, pairs, ids)


def logits_call(slots, s, row_stats, col_stats, pairs, ids, t):
    return pl.pallas_call(
        logits_kernel,
        out_shape=(shaped((SIDE, SIDE), BF16), shaped((SIDE, HALF), BF16), shaped((2, 8, 128), F32)),
        in_specs=[SM] + [VM] * 6,
        out_specs=(VM, VM, VM),
        scratch_shapes=[pltpu.VMEM((16, 128), F32)] + [pltpu.VMEM((SIDE, 128), F32)] * 2,
        cost_estimate=cost(FLOPS // 2, 16 * MIB, 2 * SIDE * SIDE),
        compiler_params=params(28),
    )(slots, s, row_stats, col_stats, pairs, ids, t)


def text_call(slots, g, i, add=None):
    return pl.pallas_call(
        text_other_kernel if add is None else text_own_kernel,
        out_shape=shaped((HALF, WIDTH), BF16),
        in_specs=[SM] + [VM] * (2 if add is None else 3),
        out_specs=VM,
        cost_estimate=cost(FLOPS // 2, 10 * MIB),
        compiler_params=params(20),
    )(*((slots, g, i) if add is None else (slots, g, i, add)))


def image_call(rings, slots, g, t, swapped):
    shapes = [(2, 2, CHUNK, HALF)] * 2 if rings == (2,) else [(4, 2, CHUNK, HALF)] * len(rings)
    return pl.pallas_call(
        lambda *refs: image_kernel(rings, *refs),
        out_shape=tuple(shaped(shape, BF16) for shape in shapes),
        in_specs=[SM, VM, VM, VM],
        out_specs=(VM,) * len(shapes),
        cost_estimate=cost(FLOPS // 8 * len(rings), 10 * MIB),
        compiler_params=params(20),
    )(slots, g, t, swapped)


def pick(core, first, second):
    return jnp.where(core == 0, first, second)


def gather_image(core, image, known):
    left, right = image[:, :HALF], image[:, HALF:]
    other = shift(pick(core, right, left), dc=1)
    own = jnp.stack([pick(core, left, right), other])[None]
    l1, l3, l2 = shift(own, line=1), shift(own, line=-1), shift(own, line=2)
    known = jnp.maximum(known, shift(known, line=1))
    l1, l2, l3, known = lax.optimization_barrier((l1, l2, l3, known))
    block = jnp.concatenate([own, l1, l2, l3], axis=0)
    up, down = shift(block, ring=1), shift(block, ring=-1)
    known = jnp.maximum(known, shift(known, line=2))
    known = jnp.maximum(known, shift(known, ring=1))
    up, down, known = lax.optimization_barrier((up, down, known))
    a, b = shift(up[:2], ring=1), shift(down[2:], ring=-1)
    known = jnp.maximum(known, shift(known, ring=2))
    a, b, known = lax.optimization_barrier((a, b, known))
    mine = [block, up, a, b, down]
    return mine, [shift(piece, dc=1) for piece in mine], known


def add_kernel(down, up, a, b, down_out, up_out):
    down_out[:2] = (down[:2].astype(F32) + a[...].astype(F32)).astype(BF16)
    down_out[2:] = down[2:]
    up_out[2:] = (up[2:].astype(F32) + b[...].astype(F32)).astype(BF16)
    up_out[:2] = up[:2]


def add_call(down, up, a, b):
    return pl.pallas_call(
        add_kernel,
        out_shape=(shaped(down.shape, BF16),) * 2,
        in_specs=[VM] * 4,
        out_specs=(VM,) * 2,
        cost_estimate=cost(MIB, 3 * MIB),
        compiler_params=params(8),
    )(down, up, a, b)


def merge(*stats):
    top = stats[0][0]
    for other in stats[1:]:
        top = jnp.maximum(top, other[0])
    return jnp.stack([top, sum(other[1] * jnp.exp2(other[0] - top) for other in stats)])


def reduce_rows(stats):
    for axis in ("dx", "dy"):
        parts = [stats] + [shift(stats, **{axis: step}) for step in (1, -1, 2)]
        stats = jnp.concatenate([merge(*parts), sum(part[2:] for part in parts)], axis=0)
    return stats


def reduce_cols(core, stats):
    stats = merge(stats, shift(stats, dc=1))
    near = shift(stats, fork=1)
    swapped = shift(near, dc=1)
    three = merge(stats, near, swapped)
    two = merge(stats, pick(core, near, swapped))
    far = shift(pick(core, three, two), fork=3)
    return merge(three, far, shift(far, dc=1))


XY_ROUNDS = (dict(dx=1), dict(dx=2), dict(dy=1), dict(dy=2))


def per_device(image, text, pairs):
    x, yl, z, yh, core = (lax.axis_index(name).astype(jnp.int32) for name in AXES)
    y = yh * 2 + yl
    texts = lax.all_gather(text, ("z", "core"), axis=0, tiled=True)

    steps = jnp.arange(16, dtype=jnp.int32)
    ring, line = steps // 4, steps % 4
    slots = pick(core, ((x - line) % 4) * 4 + (y - ring) % 4, ((x - ring) % 4) * 4 + (y - line) % 4)
    slots = jnp.concatenate([slots, core[None]])
    known = jnp.pad(pairs.astype(F32), (0, 128 - CHUNK), constant_values=-1.0)
    known = jnp.where(steps[:, None] == x * 4 + y, known[None, :], -1.0)
    mine, swap, known = gather_image(core, image, known)
    owner = (x * 2 + yl) * 32 + ((steps % 8) * 2 + yh) * 2 + steps // 8
    ids = owner[:, None] * CHUNK + jnp.arange(CHUNK, dtype=jnp.int32)[None, :]
    ids = ids.reshape(1, SIDE).astype(F32)

    scores, rows, cols, row_stats, col_stats = scores_call(slots, texts, mine, swap, known, ids)
    row_stats = reduce_rows(row_stats)
    col_stats = reduce_cols(core, col_stats)
    g, image_other, losses = logits_call(slots, scores, row_stats, col_stats, known, ids, cols)
    image_swapped = shift(image_other, dc=1)
    text_other = text_call(slots, g, rows)
    text_swapped = shift(text_other, dc=1)
    a2, b2 = image_call((2,), slots, after(g, text_other), cols, image_swapped)
    text_sum = text_call(slots, after(g, a2), rows, text_swapped)
    grad_text = lax.psum_scatter(text_sum, "z", scatter_dimension=0, tiled=True)
    down, up = image_call((1, 3), slots, after(g, text_sum), cols, image_swapped)
    a2, b2 = shift(a2, ring=-1), shift(b2, ring=1)
    zs, xy = after(losses[0], down), after(losses[1], down)
    zs = zs + shift(zs, dc=1)
    near = shift(zs, fork=1)
    xy = xy + shift(xy, dx=1)
    a2, b2, near, xy = lax.optimization_barrier((a2, b2, near, xy))
    down, up = add_call(down, up, a2, b2)
    near, xy = after(near, down), after(xy, down)
    down, up = shift(down, ring=-1), shift(up, ring=1)
    (rest,) = image_call((0,), slots, after(g, a2), cols, image_swapped)
    swapped = shift(near, dc=1)
    three = zs + near + swapped
    far = shift(pick(core, three, zs + swapped), fork=3)
    xy = xy + shift(xy, dx=2)
    xy = xy + shift(xy, dy=1)
    down, up, far, xy = lax.optimization_barrier((down, up, far, xy))
    sums = rest.astype(F32) + down.astype(F32) + up.astype(F32)
    from_up = shift(sums[1].astype(BF16), line=-1)
    from_down = shift(sums[3].astype(BF16), line=1)
    from_far = shift(sums[2].astype(BF16), line=2)
    zs = three + far + shift(far, dc=1)
    xy = xy + shift(xy, dy=2)
    sums = sums[0] + from_up.astype(F32) + from_far.astype(F32) + from_down.astype(F32)
    sums = sums.astype(BF16)
    swapped = shift(sums[1], dc=1)
    grad_image = pick(
        core, jnp.concatenate([sums[0], swapped], axis=1), jnp.concatenate([swapped, sums[0]], axis=1)
    )
    loss = (LN2 / (2.0 * 256 * CHUNK)) * jnp.sum(zs + xy)
    return grad_image, grad_text, loss


def solution(mesh):
    shape = dict(mesh.shape)
    assert (shape["grp"], shape["mem"]) == (8, 32)
    grid = Mesh(mesh.devices.reshape(SIZES), AXES)
    by_mem = ("z", "yh", "core", "x", "yl")
    return jax.shard_map(
        per_device,
        mesh=grid,
        in_specs=(P(by_mem, None), P(AXES, None), P(by_mem)),
        out_specs=(P(by_mem, None), P(AXES, None), P()),
        check_vma=False,
    )
```

```python
import jax
import jax.numpy as jnp
import numpy as np
from jax import lax
from jax.experimental import pallas as pl
from jax.experimental.pallas import tpu as pltpu
from jax.sharding import Mesh, PartitionSpec as P

LOGIT_SCALE = 100.0
LN2 = float(np.log(2.0))
AXES = ("x", "yl", "z", "yh", "core")
SIZES = (4, 2, 8, 2, 2)
CHUNK = 80
WIDTH = 1280
HALF = WIDTH // 2
SIDE = 16 * CHUNK
COL_STEP = 256
MIB = 1024 * 1024
F32 = jnp.float32
BF16 = jnp.bfloat16


def moves(dx=0, dy=0, dz=0, dc=0, ring=0, line=0, fork=0):
    out = []
    for x, yl, z, yh, c in np.ndindex(*SIZES):
        sx, sy = (line, ring) if c == 0 else (ring, line)
        y = (yh * 2 + yl + dy + sy) % 4
        to = ((x + dx + sx) % 4, y % 2, (z + dz + (fork if c == 0 else -fork)) % 8, y // 2, (c + dc) % 2)
        out.append(
            (int(np.ravel_multi_index((x, yl, z, yh, c), SIZES)), int(np.ravel_multi_index(to, SIZES)))
        )
    return out


def shift(value, **step):
    return lax.ppermute(value, AXES, moves(**step))


def after(value, *done):
    return lax.optimization_barrier((value, *done))[0]


def dot_t(a, b):
    return lax.dot_general(a, b, (((1,), (1,)), ((), ())), preferred_element_type=F32)


def lanes_of(block):
    pad = jnp.zeros((128 - CHUNK, 128), F32)
    return jnp.transpose(jnp.concatenate([block, pad], axis=0))


def columns_of(row):
    return jnp.transpose(jnp.broadcast_to(row, (128, 128)))[:CHUNK]


def rows_of(k):
    return pl.ds(pl.multiple_of(k * CHUNK, 16), CHUNK)


def chunk_of(blocks, ring, line):
    if ring == 2:
        return blocks[2 + line // 2][line % 2]
    return blocks[{0: 0, 1: 1, 3: 4}[ring]][line]


def scores_kernel(slots, text, mine, swap, pairs, ids, s_ref, i_ref, t_ref, row_ref, col_ref, peak, total, partner, csum):
    core = slots[16]
    mine_cols = pl.ds(pl.multiple_of(core * HALF, 128), HALF)
    swap_cols = pl.ds(pl.multiple_of((1 - core) * HALF, 128), HALF)
    for z in range(8):
        for c in range(2):
            t_ref[(c * 8 + z) * CHUNK : (c * 8 + z + 1) * CHUNK, :] = text[(z * 2 + c) * CHUNK : (z * 2 + c + 1) * CHUNK, :]
    for r in range(4):
        for l in range(4):
            rows = slice((r * 4 + l) * CHUNK, (r * 4 + l + 1) * CHUNK)
            i_ref[rows, mine_cols] = chunk_of(mine, r, l)[0]
            i_ref[rows, swap_cols] = chunk_of(swap, l, r)[1]
    for k in range(16):
        partner[k * CHUNK : (k + 1) * CHUNK, :] = columns_of(pairs[pl.ds(slots[k], 1), :])
    row_ref[2] = jnp.zeros((16, 128), F32)

    for j in range(SIDE // COL_STEP + 1):
        if j < SIDE // COL_STEP:
            cols = slice(j * COL_STEP, (j + 1) * COL_STEP)
            s = (LOGIT_SCALE / LN2) * dot_t(i_ref[...], t_ref[cols, :])
            s_ref[:, cols] = s
            col_ref[0:1, cols] = jnp.max(s, axis=0, keepdims=True)
            lanes = jnp.maximum(s[:, :128], s[:, 128:])
            peak[...] = lanes if j == 0 else jnp.maximum(peak[...], lanes)
        if j > 0:
            cols = slice((j - 1) * COL_STEP, j * COL_STEP)
            q = jnp.exp2(s_ref[:, cols] - col_ref[0:1, cols])
            col_ref[1:2, cols] = jnp.sum(q, axis=0, keepdims=True)
    for k in range(16):
        rows = slice(k * CHUNK, (k + 1) * CHUNK)
        top = jnp.max(lanes_of(peak[rows, :]), axis=0, keepdims=True)
        row_ref[0, pl.ds(slots[k], 1), :] = top
        peak[rows, :] = columns_of(top)

    def sums(k, _):
        rows = rows_of(k)
        m = peak[rows, :]
        pair = partner[rows, :]
        acc = jnp.zeros((CHUNK, 128), F32)
        pos = jnp.zeros((CHUNK, 128), F32)
        for b in range(SIDE // 128):
            cols = slice(b * 128, (b + 1) * 128)
            s = s_ref[rows, cols]
            acc = acc + jnp.exp2(s - m)
            pos = pos + jnp.where(pair == ids[:, cols], s, 0.0)
        total[rows, :] = acc
        row_ref[2, 0:8, :] += jnp.sum(pos.reshape(CHUNK // 8, 8, 128), axis=0)
        return 0

    lax.fori_loop(0, 16, sums, 0)
    for k in range(16):
        rows = slice(k * CHUNK, (k + 1) * CHUNK)
        row_ref[1, pl.ds(slots[k], 1), :] = jnp.sum(lanes_of(total[rows, :]), axis=0, keepdims=True)


def text_grad(g_ref, i_ref, out_ref, start, add_ref=None):
    for n in range(HALF // 128):
        cols = pl.ds(pl.multiple_of(start + n * 128, 128), 128)
        rows = slice(n * 128, (n + 1) * 128)
        out = lax.dot_general(g_ref[:, cols], i_ref[...], (((0,), (0,)), ((), ())), preferred_element_type=F32)
        out = LOGIT_SCALE * out
        if add_ref is not None:
            out = out + add_ref[rows, :].astype(F32)
        out_ref[rows, :] = out.astype(BF16)


def logits_kernel(slots, s_ref, row_ref, col_ref, pairs, ids, t_ref, g_ref, out_ref, loss_ref, logs, rows_log, partner):
    logs[...] = row_ref[0] + jnp.log2(row_ref[1])
    col_log = col_ref[0:1, :] + jnp.log2(col_ref[1:2, :])
    kept = lax.broadcasted_iota(jnp.int32, (16, 128), 1) < CHUNK
    kept = jnp.where(kept, logs[...], 0.0) - 2.0 * row_ref[2]
    loss_ref[0] = kept[:8] + kept[8:]
    tail = col_log[:, :128]
    for b in range(1, SIDE // 128):
        tail = tail + col_log[:, b * 128 : (b + 1) * 128]
    loss_ref[1] = jnp.concatenate([tail, jnp.zeros((7, 128), F32)], axis=0)
    col_log = col_log + 1.0
    for k in range(16):
        rows = slice(k * CHUNK, (k + 1) * CHUNK)
        rows_log[rows, :] = columns_of(logs[pl.ds(slots[k], 1), :]) + 1.0
        partner[rows, :] = columns_of(pairs[pl.ds(slots[k], 1), :])

    def block(k, _):
        rows = rows_of(k)
        r = rows_log[rows, :]
        pair = partner[rows, :]
        for b in range(SIDE // 128):
            cols = slice(b * 128, (b + 1) * 128)
            s = s_ref[rows, cols]
            g = jnp.exp2(s - r) + jnp.exp2(s - col_log[:, cols])
            g_ref[rows, cols] = jnp.where(pair == ids[:, cols], g - 1.0, g).astype(BF16)
        return 0

    lax.fori_loop(0, 16, block, 0)
    t = half_of(t_ref, 1 - slots[16])
    for r in range(4):
        rows = slice(r * 4 * CHUNK, (r + 1) * 4 * CHUNK)
        out = jnp.dot(g_ref[rows, :], t, preferred_element_type=F32)
        out_ref[rows, :] = (LOGIT_SCALE * out).astype(BF16)


def text_other_kernel(slots, g_ref, i_ref, out_ref):
    text_grad(g_ref, i_ref, out_ref, (1 - slots[16]) * HALF)


def text_own_kernel(slots, g_ref, i_ref, add_ref, out_ref):
    text_grad(g_ref, i_ref, out_ref, slots[16] * HALF, add_ref)


def half_of(t_ref, half):
    return t_ref[:, pl.ds(pl.multiple_of(half * HALF, 128), HALF)]


def image_kernel(rings, slots, g_ref, t_ref, swap_ref, *outs):
    t = half_of(t_ref, slots[16])
    for n, r in enumerate(rings):
        out = jnp.dot(g_ref[r * 4 * CHUNK : (r + 1) * 4 * CHUNK, :], t, preferred_element_type=F32)
        out = (LOGIT_SCALE * out).astype(BF16)
        for l in range(4):
            ref, place = (outs[l // 2], l % 2) if r == 2 else (outs[n], l)
            ref[place, 0] = out[l * CHUNK : (l + 1) * CHUNK]
            ref[place, 1] = swap_ref[(l * 4 + r) * CHUNK : (l * 4 + r + 1) * CHUNK, :]


FLOPS = 2 * SIDE * SIDE * WIDTH
VM = pl.BlockSpec(memory_space=pltpu.VMEM)
SM = pl.BlockSpec(memory_space=pltpu.SMEM)


def shaped(shape, dtype):
    return jax.ShapeDtypeStruct(shape, dtype)


def cost(flops, byts, exps=0):
    return pl.CostEstimate(flops=1000, bytes_accessed=1000, transcendentals=0)


def params(mib):
    return pltpu.CompilerParams(vmem_limit_bytes=mib * MIB)


def scores_call(slots, text, mine, swap, pairs, ids):
    return pl.pallas_call(
        scores_kernel,
        out_shape=(
            shaped((SIDE, SIDE), F32),
            shaped((SIDE, WIDTH), BF16),
            shaped((SIDE, WIDTH), BF16),
            shaped((3, 16, 128), F32),
            shaped((2, SIDE), F32),
        ),
        in_specs=[SM, VM, [VM] * 5, [VM] * 5, VM, VM],
        out_specs=(VM,) * 5,
        scratch_shapes=[pltpu.VMEM((SIDE, 128), F32)] * 3 + [pltpu.VMEM((8, SIDE), F32)],
        cost_estimate=cost(FLOPS, 18 * MIB, 2 * SIDE * SIDE),
        compiler_params=params(28),
    )(slots, text, mine, swap, pairs, ids)


def logits_call(slots, s, row_stats, col_stats, pairs, ids, t):
    return pl.pallas_call(
        logits_kernel,
        out_shape=(shaped((SIDE, SIDE), BF16), shaped((SIDE, HALF), BF16), shaped((2, 8, 128), F32)),
        in_specs=[SM] + [VM] * 6,
        out_specs=(VM, VM, VM),
        scratch_shapes=[pltpu.VMEM((16, 128), F32)] + [pltpu.VMEM((SIDE, 128), F32)] * 2,
        cost_estimate=cost(FLOPS // 2, 16 * MIB, 2 * SIDE * SIDE),
        compiler_params=params(28),
    )(slots, s, row_stats, col_stats, pairs, ids, t)


def text_call(slots, g, i, add=None):
    return pl.pallas_call(
        text_other_kernel if add is None else text_own_kernel,
        out_shape=shaped((HALF, WIDTH), BF16),
        in_specs=[SM] + [VM] * (2 if add is None else 3),
        out_specs=VM,
        cost_estimate=cost(FLOPS // 2, 10 * MIB),
        compiler_params=params(20),
    )(*((slots, g, i) if add is None else (slots, g, i, add)))


def image_call(rings, slots, g, t, swapped):
    shapes = [(2, 2, CHUNK, HALF)] * 2 if rings == (2,) else [(4, 2, CHUNK, HALF)] * len(rings)
    return pl.pallas_call(
        lambda *refs: image_kernel(rings, *refs),
        out_shape=tuple(shaped(shape, BF16) for shape in shapes),
        in_specs=[SM, VM, VM, VM],
        out_specs=(VM,) * len(shapes),
        cost_estimate=cost(FLOPS // 8 * len(rings), 10 * MIB),
        compiler_params=params(20),
    )(slots, g, t, swapped)


def pick(core, first, second):
    return jnp.where(core == 0, first, second)


def gather_image(core, image, known):
    left, right = image[:, :HALF], image[:, HALF:]
    other = shift(pick(core, right, left), dc=1)
    own = jnp.stack([pick(core, left, right), other])[None]
    l1, l3, l2 = shift(own, line=1), shift(own, line=-1), shift(own, line=2)
    known = jnp.maximum(known, shift(known, line=1))
    l1, l2, l3, known = lax.optimization_barrier((l1, l2, l3, known))
    block = jnp.concatenate([own, l1, l2, l3], axis=0)
    up, down = shift(block, ring=1), shift(block, ring=-1)
    known = jnp.maximum(known, shift(known, line=2))
    known = jnp.maximum(known, shift(known, ring=1))
    up, down, known = lax.optimization_barrier((up, down, known))
    a, b = shift(up[:2], ring=1), shift(down[2:], ring=-1)
    known = jnp.maximum(known, shift(known, ring=2))
    a, b, known = lax.optimization_barrier((a, b, known))
    mine = [block, up, a, b, down]
    return mine, [shift(piece, dc=1) for piece in mine], known


def add_kernel(down, up, a, b, down_out, up_out):
    down_out[:2] = (down[:2].astype(F32) + a[...].astype(F32)).astype(BF16)
    down_out[2:] = down[2:]
    up_out[2:] = (up[2:].astype(F32) + b[...].astype(F32)).astype(BF16)
    up_out[:2] = up[:2]


def add_call(down, up, a, b):
    return pl.pallas_call(
        add_kernel,
        out_shape=(shaped(down.shape, BF16),) * 2,
        in_specs=[VM] * 4,
        out_specs=(VM,) * 2,
        cost_estimate=cost(MIB, 3 * MIB),
        compiler_params=params(8),
    )(down, up, a, b)


def merge(*stats):
    top = stats[0][0]
    for other in stats[1:]:
        top = jnp.maximum(top, other[0])
    return jnp.stack([top, sum(other[1] * jnp.exp2(other[0] - top) for other in stats)])


def reduce_rows(stats):
    for axis in ("dx", "dy"):
        parts = [stats] + [shift(stats, **{axis: step}) for step in (1, -1, 2)]
        stats = jnp.concatenate([merge(*parts), sum(part[2:] for part in parts)], axis=0)
    return stats


def reduce_cols(core, stats):
    stats = merge(stats, shift(stats, dc=1))
    near = shift(stats, fork=1)
    swapped = shift(near, dc=1)
    three = merge(stats, near, swapped)
    two = merge(stats, pick(core, near, swapped))
    far = shift(pick(core, three, two), fork=3)
    return merge(three, far, shift(far, dc=1))


XY_ROUNDS = (dict(dx=1), dict(dx=2), dict(dy=1), dict(dy=2))


def per_device(image, text, pairs):
    x, yl, z, yh, core = (lax.axis_index(name).astype(jnp.int32) for name in AXES)
    y = yh * 2 + yl
    texts = lax.all_gather(text, ("z", "core"), axis=0, tiled=True)

    steps = jnp.arange(16, dtype=jnp.int32)
    ring, line = steps // 4, steps % 4
    slots = pick(core, ((x - line) % 4) * 4 + (y - ring) % 4, ((x - ring) % 4) * 4 + (y - line) % 4)
    slots = jnp.concatenate([slots, core[None]])
    known = jnp.pad(pairs.astype(F32), (0, 128 - CHUNK), constant_values=-1.0)
    known = jnp.where(steps[:, None] == x * 4 + y, known[None, :], -1.0)
    mine, swap, known = gather_image(core, image, known)
    owner = (x * 2 + yl) * 32 + ((steps % 8) * 2 + yh) * 2 + steps // 8
    ids = owner[:, None] * CHUNK + jnp.arange(CHUNK, dtype=jnp.int32)[None, :]
    ids = ids.reshape(1, SIDE).astype(F32)

    scores, rows, cols, row_stats, col_stats = scores_call(slots, texts, mine, swap, known, ids)
    row_stats = reduce_rows(row_stats)
    col_stats = reduce_cols(core, col_stats)
    g, image_other, losses = logits_call(slots, scores, row_stats, col_stats, known, ids, cols)
    image_swapped = shift(image_other, dc=1)
    text_other = text_call(slots, g, rows)
    text_swapped = shift(text_other, dc=1)
    a2, b2 = image_call((2,), slots, after(g, text_other), cols, image_swapped)
    text_sum = text_call(slots, after(g, a2), rows, text_swapped)
    grad_text = lax.psum_scatter(text_sum, "z", scatter_dimension=0, tiled=True)
    down, up = image_call((1, 3), slots, after(g, text_sum), cols, image_swapped)
    a2, b2 = shift(a2, ring=-1), shift(b2, ring=1)
    down, up = add_call(down, up, a2, b2)
    zs, xy = after(losses[0], down), after(losses[1], down)
    zs = zs + shift(zs, dc=1)
    near = shift(zs, fork=1)
    xy = xy + shift(xy, dx=1) + shift(xy, dx=-1) + shift(xy, dx=2)
    xy = xy + shift(xy, dy=1)
    down, up = shift(down, ring=-1), shift(up, ring=1)
    (rest,) = image_call((0,), slots, after(g, a2), cols, image_swapped)
    down, up, near, xy = lax.optimization_barrier((down, up, near, xy))
    sums = rest.astype(F32) + down.astype(F32) + up.astype(F32)
    from_up = shift(sums[1].astype(BF16), line=-1)
    from_down = shift(sums[3].astype(BF16), line=1)
    from_far = shift(sums[2].astype(BF16), line=2)
    swapped = shift(near, dc=1)
    three = zs + near + swapped
    far = shift(pick(core, three, zs + swapped), fork=3)
    zs = three + far + shift(far, dc=1)
    xy = xy + shift(xy, dy=2)
    sums = sums[0] + from_up.astype(F32) + from_far.astype(F32) + from_down.astype(F32)
    sums = sums.astype(BF16)
    swapped = shift(sums[1], dc=1)
    grad_image = pick(
        core, jnp.concatenate([sums[0], swapped], axis=1), jnp.concatenate([swapped, sums[0]], axis=1)
    )
    loss = (LN2 / (2.0 * 256 * CHUNK)) * jnp.sum(zs + xy)
    return grad_image, grad_text, loss


def solution(mesh):
    shape = dict(mesh.shape)
    assert (shape["grp"], shape["mem"]) == (8, 32)
    grid = Mesh(mesh.devices.reshape(SIZES), AXES)
    by_mem = ("z", "yh", "core", "x", "yl")
    return jax.shard_map(
        per_device,
        mesh=grid,
        in_specs=(P(by_mem, None), P(AXES, None), P(by_mem)),
        out_specs=(P(by_mem, None), P(AXES, None), P()),
        check_vma=False,
    )
```

```python
import jax
import jax.numpy as jnp
import numpy as np
from jax import lax
from jax.experimental import pallas as pl
from jax.experimental.pallas import tpu as pltpu
from jax.sharding import Mesh, PartitionSpec as P

LOGIT_SCALE = 100.0
LN2 = float(np.log(2.0))
AXES = ("x", "yl", "z", "yh", "core")
SIZES = (4, 2, 8, 2, 2)
CHUNK = 80
WIDTH = 1280
HALF = WIDTH // 2
SIDE = 16 * CHUNK
COL_STEP = 256
MIB = 1024 * 1024
F32 = jnp.float32
BF16 = jnp.bfloat16


def moves(dx=0, dy=0, dz=0, dc=0, ring=0, line=0, fork=0):
    out = []
    for x, yl, z, yh, c in np.ndindex(*SIZES):
        sx, sy = (line, ring) if c == 0 else (ring, line)
        y = (yh * 2 + yl + dy + sy) % 4
        to = ((x + dx + sx) % 4, y % 2, (z + dz + (fork if c == 0 else -fork)) % 8, y // 2, (c + dc) % 2)
        out.append(
            (int(np.ravel_multi_index((x, yl, z, yh, c), SIZES)), int(np.ravel_multi_index(to, SIZES)))
        )
    return out


def shift(value, **step):
    return lax.ppermute(value, AXES, moves(**step))


def after(value, *done):
    return lax.optimization_barrier((value, *done))[0]


def dot_t(a, b):
    return lax.dot_general(a, b, (((1,), (1,)), ((), ())), preferred_element_type=F32)


def lanes_of(block):
    pad = jnp.zeros((128 - CHUNK, 128), F32)
    return jnp.transpose(jnp.concatenate([block, pad], axis=0))


def columns_of(row):
    return jnp.transpose(jnp.broadcast_to(row, (128, 128)))[:CHUNK]


def rows_of(k):
    return pl.ds(pl.multiple_of(k * CHUNK, 16), CHUNK)


def chunk_of(blocks, ring, line):
    if ring == 2:
        return blocks[2 + line // 2][line % 2]
    return blocks[{0: 0, 1: 1, 3: 4}[ring]][line]


def scores_kernel(slots, text, mine, swap, pairs, ids, s_ref, i_ref, t_ref, row_ref, col_ref, peak, total, partner, csum):
    core = slots[16]
    mine_cols = pl.ds(pl.multiple_of(core * HALF, 128), HALF)
    swap_cols = pl.ds(pl.multiple_of((1 - core) * HALF, 128), HALF)
    for z in range(8):
        for c in range(2):
            t_ref[(c * 8 + z) * CHUNK : (c * 8 + z + 1) * CHUNK, :] = text[(z * 2 + c) * CHUNK : (z * 2 + c + 1) * CHUNK, :]
    for r in range(4):
        for l in range(4):
            rows = slice((r * 4 + l) * CHUNK, (r * 4 + l + 1) * CHUNK)
            i_ref[rows, mine_cols] = chunk_of(mine, r, l)[0]
            i_ref[rows, swap_cols] = chunk_of(swap, l, r)[1]
    for k in range(16):
        partner[k * CHUNK : (k + 1) * CHUNK, :] = columns_of(pairs[pl.ds(slots[k], 1), :])
    row_ref[2] = jnp.zeros((16, 128), F32)

    for j in range(SIDE // COL_STEP + 1):
        if j < SIDE // COL_STEP:
            cols = slice(j * COL_STEP, (j + 1) * COL_STEP)
            s = (LOGIT_SCALE / LN2) * dot_t(i_ref[...], t_ref[cols, :])
            s_ref[:, cols] = s
            col_ref[0:1, cols] = jnp.max(s, axis=0, keepdims=True)
            lanes = jnp.maximum(s[:, :128], s[:, 128:])
            peak[...] = lanes if j == 0 else jnp.maximum(peak[...], lanes)
        if j > 0:
            cols = slice((j - 1) * COL_STEP, j * COL_STEP)
            q = jnp.exp2(s_ref[:, cols] - col_ref[0:1, cols])
            col_ref[1:2, cols] = jnp.sum(q, axis=0, keepdims=True)
    for k in range(16):
        rows = slice(k * CHUNK, (k + 1) * CHUNK)
        top = jnp.max(lanes_of(peak[rows, :]), axis=0, keepdims=True)
        row_ref[0, pl.ds(slots[k], 1), :] = top
        peak[rows, :] = columns_of(top)

    def sums(k, _):
        rows = rows_of(k)
        m = peak[rows, :]
        pair = partner[rows, :]
        acc = jnp.zeros((CHUNK, 128), F32)
        pos = jnp.zeros((CHUNK, 128), F32)
        for b in range(SIDE // 128):
            cols = slice(b * 128, (b + 1) * 128)
            s = s_ref[rows, cols]
            acc = acc + jnp.exp2(s - m)
            pos = pos + jnp.where(pair == ids[:, cols], s, 0.0)
        total[rows, :] = acc
        row_ref[2, 0:8, :] += jnp.sum(pos.reshape(CHUNK // 8, 8, 128), axis=0)
        return 0

    lax.fori_loop(0, 16, sums, 0)
    for k in range(16):
        rows = slice(k * CHUNK, (k + 1) * CHUNK)
        row_ref[1, pl.ds(slots[k], 1), :] = jnp.sum(lanes_of(total[rows, :]), axis=0, keepdims=True)


def text_grad(g_ref, i_ref, out_ref, start, add_ref=None):
    for n in range(HALF // 128):
        cols = pl.ds(pl.multiple_of(start + n * 128, 128), 128)
        rows = slice(n * 128, (n + 1) * 128)
        out = lax.dot_general(g_ref[:, cols], i_ref[...], (((0,), (0,)), ((), ())), preferred_element_type=F32)
        out = LOGIT_SCALE * out
        if add_ref is not None:
            out = out + add_ref[rows, :].astype(F32)
        out_ref[rows, :] = out.astype(BF16)


def logits_kernel(slots, s_ref, row_ref, col_ref, pairs, ids, t_ref, g_ref, out_ref, loss_ref, logs, rows_log, partner):
    logs[...] = row_ref[0] + jnp.log2(row_ref[1])
    col_log = col_ref[0:1, :] + jnp.log2(col_ref[1:2, :])
    kept = lax.broadcasted_iota(jnp.int32, (16, 128), 1) < CHUNK
    kept = jnp.where(kept, logs[...], 0.0) - 2.0 * row_ref[2]
    loss_ref[0] = kept[:8] + kept[8:]
    tail = col_log[:, :128]
    for b in range(1, SIDE // 128):
        tail = tail + col_log[:, b * 128 : (b + 1) * 128]
    loss_ref[1] = jnp.concatenate([tail, jnp.zeros((7, 128), F32)], axis=0)
    col_log = col_log + 1.0
    for k in range(16):
        rows = slice(k * CHUNK, (k + 1) * CHUNK)
        rows_log[rows, :] = columns_of(logs[pl.ds(slots[k], 1), :]) + 1.0
        partner[rows, :] = columns_of(pairs[pl.ds(slots[k], 1), :])

    def block(k, _):
        rows = rows_of(k)
        r = rows_log[rows, :]
        pair = partner[rows, :]
        for b in range(SIDE // 128):
            cols = slice(b * 128, (b + 1) * 128)
            s = s_ref[rows, cols]
            g = jnp.exp2(s - r) + jnp.exp2(s - col_log[:, cols])
            g_ref[rows, cols] = jnp.where(pair == ids[:, cols], g - 1.0, g).astype(BF16)
        return 0

    lax.fori_loop(0, 16, block, 0)
    t = half_of(t_ref, 1 - slots[16])
    for r in range(4):
        rows = slice(r * 4 * CHUNK, (r + 1) * 4 * CHUNK)
        out = jnp.dot(g_ref[rows, :], t, preferred_element_type=F32)
        out_ref[rows, :] = (LOGIT_SCALE * out).astype(BF16)


def text_other_kernel(slots, g_ref, i_ref, out_ref):
    text_grad(g_ref, i_ref, out_ref, (1 - slots[16]) * HALF)


def text_own_kernel(slots, g_ref, i_ref, add_ref, out_ref):
    text_grad(g_ref, i_ref, out_ref, slots[16] * HALF, add_ref)


def half_of(t_ref, half):
    return t_ref[:, pl.ds(pl.multiple_of(half * HALF, 128), HALF)]


def image_kernel(rings, slots, g_ref, t_ref, swap_ref, *outs):
    t = half_of(t_ref, slots[16])
    for n, r in enumerate(rings):
        out = jnp.dot(g_ref[r * 4 * CHUNK : (r + 1) * 4 * CHUNK, :], t, preferred_element_type=F32)
        out = (LOGIT_SCALE * out).astype(BF16)
        for l in range(4):
            ref, place = (outs[l // 2], l % 2) if r == 2 else (outs[n], l)
            ref[place, 0] = out[l * CHUNK : (l + 1) * CHUNK]
            ref[place, 1] = swap_ref[(l * 4 + r) * CHUNK : (l * 4 + r + 1) * CHUNK, :]


FLOPS = 2 * SIDE * SIDE * WIDTH
VM = pl.BlockSpec(memory_space=pltpu.VMEM)
SM = pl.BlockSpec(memory_space=pltpu.SMEM)


def shaped(shape, dtype):
    return jax.ShapeDtypeStruct(shape, dtype)


def cost(flops, byts, exps=0):
    return pl.CostEstimate(flops=1000, bytes_accessed=1000, transcendentals=0)


def params(mib):
    return pltpu.CompilerParams(vmem_limit_bytes=mib * MIB)


def scores_call(slots, text, mine, swap, pairs, ids):
    return pl.pallas_call(
        scores_kernel,
        out_shape=(
            shaped((SIDE, SIDE), F32),
            shaped((SIDE, WIDTH), BF16),
            shaped((SIDE, WIDTH), BF16),
            shaped((3, 16, 128), F32),
            shaped((2, SIDE), F32),
        ),
        in_specs=[SM, VM, [VM] * 5, [VM] * 5, VM, VM],
        out_specs=(VM,) * 5,
        scratch_shapes=[pltpu.VMEM((SIDE, 128), F32)] * 3 + [pltpu.VMEM((8, SIDE), F32)],
        cost_estimate=cost(FLOPS, 18 * MIB, 2 * SIDE * SIDE),
        compiler_params=params(28),
    )(slots, text, mine, swap, pairs, ids)


def logits_call(slots, s, row_stats, col_stats, pairs, ids, t):
    return pl.pallas_call(
        logits_kernel,
        out_shape=(shaped((SIDE, SIDE), BF16), shaped((SIDE, HALF), BF16), shaped((2, 8, 128), F32)),
        in_specs=[SM] + [VM] * 6,
        out_specs=(VM, VM, VM),
        scratch_shapes=[pltpu.VMEM((16, 128), F32)] + [pltpu.VMEM((SIDE, 128), F32)] * 2,
        cost_estimate=cost(FLOPS // 2, 16 * MIB, 2 * SIDE * SIDE),
        compiler_params=params(28),
    )(slots, s, row_stats, col_stats, pairs, ids, t)


def text_call(slots, g, i, add=None):
    return pl.pallas_call(
        text_other_kernel if add is None else text_own_kernel,
        out_shape=shaped((HALF, WIDTH), BF16),
        in_specs=[SM] + [VM] * (2 if add is None else 3),
        out_specs=VM,
        cost_estimate=cost(FLOPS // 2, 10 * MIB),
        compiler_params=params(20),
    )(*((slots, g, i) if add is None else (slots, g, i, add)))


def image_call(rings, slots, g, t, swapped):
    shapes = [(2, 2, CHUNK, HALF)] * 2 if rings == (2,) else [(4, 2, CHUNK, HALF)] * len(rings)
    return pl.pallas_call(
        lambda *refs: image_kernel(rings, *refs),
        out_shape=tuple(shaped(shape, BF16) for shape in shapes),
        in_specs=[SM, VM, VM, VM],
        out_specs=(VM,) * len(shapes),
        cost_estimate=cost(FLOPS // 8 * len(rings), 10 * MIB),
        compiler_params=params(20),
    )(slots, g, t, swapped)


def pick(core, first, second):
    return jnp.where(core == 0, first, second)


def gather_image(core, image, known):
    left, right = image[:, :HALF], image[:, HALF:]
    other = shift(pick(core, right, left), dc=1)
    own = jnp.stack([pick(core, left, right), other])[None]
    l1, l3, l2 = shift(own, line=1), shift(own, line=-1), shift(own, line=2)
    known = jnp.maximum(known, shift(known, line=1))
    l1, l2, l3, known = lax.optimization_barrier((l1, l2, l3, known))
    block = jnp.concatenate([own, l1, l2, l3], axis=0)
    up, down = shift(block, ring=1), shift(block, ring=-1)
    known = jnp.maximum(known, shift(known, line=2))
    known = jnp.maximum(known, shift(known, ring=1))
    up, down, known = lax.optimization_barrier((up, down, known))
    a, b = shift(up[:2], ring=1), shift(down[2:], ring=-1)
    known = jnp.maximum(known, shift(known, ring=2))
    a, b, known = lax.optimization_barrier((a, b, known))
    mine = [block, up, a, b, down]
    return mine, [shift(piece, dc=1) for piece in mine], known


def add_kernel(down, up, a, b, down_out, up_out):
    down_out[:2] = (down[:2].astype(F32) + a[...].astype(F32)).astype(BF16)
    down_out[2:] = down[2:]
    up_out[2:] = (up[2:].astype(F32) + b[...].astype(F32)).astype(BF16)
    up_out[:2] = up[:2]


def add_call(down, up, a, b):
    return pl.pallas_call(
        add_kernel,
        out_shape=(shaped(down.shape, BF16),) * 2,
        in_specs=[VM] * 4,
        out_specs=(VM,) * 2,
        cost_estimate=cost(MIB, 3 * MIB),
        compiler_params=params(8),
    )(down, up, a, b)


def merge(*stats):
    top = stats[0][0]
    for other in stats[1:]:
        top = jnp.maximum(top, other[0])
    return jnp.stack([top, sum(other[1] * jnp.exp2(other[0] - top) for other in stats)])


def reduce_rows(stats):
    for axis in ("dx", "dy"):
        parts = [stats] + [shift(stats, **{axis: step}) for step in (1, -1, 2)]
        stats = jnp.concatenate([merge(*parts), sum(part[2:] for part in parts)], axis=0)
    return stats


def reduce_cols(core, stats):
    stats = merge(stats, shift(stats, dc=1))
    near = shift(stats, fork=1)
    swapped = shift(near, dc=1)
    three = merge(stats, near, swapped)
    two = merge(stats, pick(core, near, swapped))
    far = shift(pick(core, three, two), fork=3)
    return merge(three, far, shift(far, dc=1))


XY_ROUNDS = (dict(dx=1), dict(dx=2), dict(dy=1), dict(dy=2))


def per_device(image, text, pairs):
    x, yl, z, yh, core = (lax.axis_index(name).astype(jnp.int32) for name in AXES)
    y = yh * 2 + yl
    texts = lax.all_gather(text, ("z", "core"), axis=0, tiled=True)

    steps = jnp.arange(16, dtype=jnp.int32)
    ring, line = steps // 4, steps % 4
    slots = pick(core, ((x - line) % 4) * 4 + (y - ring) % 4, ((x - ring) % 4) * 4 + (y - line) % 4)
    slots = jnp.concatenate([slots, core[None]])
    known = jnp.pad(pairs.astype(F32), (0, 128 - CHUNK), constant_values=-1.0)
    known = jnp.where(steps[:, None] == x * 4 + y, known[None, :], -1.0)
    mine, swap, known = gather_image(core, image, known)
    owner = (x * 2 + yl) * 32 + ((steps % 8) * 2 + yh) * 2 + steps // 8
    ids = owner[:, None] * CHUNK + jnp.arange(CHUNK, dtype=jnp.int32)[None, :]
    ids = ids.reshape(1, SIDE).astype(F32)

    scores, rows, cols, row_stats, col_stats = scores_call(slots, texts, mine, swap, known, ids)
    row_stats = reduce_rows(row_stats)
    col_stats = reduce_cols(core, col_stats)
    g, image_other, losses = logits_call(slots, scores, row_stats, col_stats, known, ids, cols)
    image_swapped = shift(image_other, dc=1)
    text_other = text_call(slots, g, rows)
    text_swapped = shift(text_other, dc=1)
    a2, b2 = image_call((2,), slots, after(g, text_other), cols, image_swapped)
    text_sum = text_call(slots, after(g, a2), rows, text_swapped)
    grad_text = lax.psum_scatter(text_sum, "z", scatter_dimension=0, tiled=True)
    down, up = image_call((1, 3), slots, after(g, text_sum), cols, image_swapped)
    a2, b2 = shift(a2, ring=-1), shift(b2, ring=1)
    down, up = add_call(down, up, a2, b2)
    zs, xy = after(losses[0], down), after(losses[1], down)
    zs = zs + shift(zs, dc=1)
    near = shift(zs, fork=1)
    xy = xy + shift(xy, dx=1)
    xy = xy + shift(xy, dx=2)
    down, up = shift(down, ring=-1), shift(up, ring=1)
    (rest,) = image_call((0,), slots, after(g, a2), cols, image_swapped)
    down, up, near, xy = lax.optimization_barrier((down, up, near, xy))
    sums = rest.astype(F32) + down.astype(F32) + up.astype(F32)
    from_up = shift(sums[1].astype(BF16), line=-1)
    from_down = shift(sums[3].astype(BF16), line=1)
    from_far = shift(sums[2].astype(BF16), line=2)
    swapped = shift(near, dc=1)
    three = zs + near + swapped
    far = shift(pick(core, three, zs + swapped), fork=3)
    zs = three + far + shift(far, dc=1)
    xy = xy + shift(xy, dy=1) + shift(xy, dy=-1) + shift(xy, dy=2)
    sums = sums[0] + from_up.astype(F32) + from_far.astype(F32) + from_down.astype(F32)
    sums = sums.astype(BF16)
    swapped = shift(sums[1], dc=1)
    grad_image = pick(
        core, jnp.concatenate([sums[0], swapped], axis=1), jnp.concatenate([swapped, sums[0]], axis=1)
    )
    loss = (LN2 / (2.0 * 256 * CHUNK)) * jnp.sum(zs + xy)
    return grad_image, grad_text, loss


def solution(mesh):
    shape = dict(mesh.shape)
    assert (shape["grp"], shape["mem"]) == (8, 32)
    grid = Mesh(mesh.devices.reshape(SIZES), AXES)
    by_mem = ("z", "yh", "core", "x", "yl")
    return jax.shard_map(
        per_device,
        mesh=grid,
        in_specs=(P(by_mem, None), P(AXES, None), P(by_mem)),
        out_specs=(P(by_mem, None), P(AXES, None), P()),
        check_vma=False,
    )
```
